512 devices in a mesh: dp: 64 (over y, z), tensor: 8 (over x, core).
Axes of the slice: x: 4, y: 4, z: 16, core: 2. Of those that a mesh axis runs over, the one named last changes fastest.
Arguments:
- layer_inputs: bfloat16 [3, 16384, 4096], P(None, 'dp', 'tensor'), may hold values from -8 to 8
- layer_outgrads: bfloat16 [3, 16384, 2048], P(None, 'dp', 'tensor'), may hold values from -0.125 to 0.125
- doc_starts: int32 [64, 8], P('dp'), may hold values from 0 to 256, as said below
- row_tokens: int32 [64], P('dp'), may hold values from 64 to 256, as said below
- doc_patient: int32 [64, 8], P('dp'), may hold values from 0 to 127
Outputs:
- weight_grad: float32 [4096, 2048], P('dp', 'tensor')
- doc_scale: float32 [64, 8], P('dp')
The draws below stay inside these ranges and needn't reach their ends.
Inputs may be any that keep to these rules, and one draw needn't show every extreme that they name: doc_starts[r, 0] = 0 and each row's starts never fall; slot d covers positions doc_starts[r, d] to doc_starts[r, d + 1] - 1, the last slot up to row_tokens[r] - 1; a nonempty slot holds 16 to 64 tokens and every row has one of exactly 64; empty slots start at row_tokens[r]. row_tokens[r] is the end of row r's last nonempty document; later positions are padding.
All inputs are finite; a program needn't handle non-finite values.
Results may differ from the reference program's by a relative error of at most 0.0013.
Values may be sent and summed in bfloat16 or wider, within the bound.
A program may use at most 64 MiB of HBM per device.

```python
import math
import jax
import jax.numpy as jnp
from jax import lax

D = 4096
LAYERS = 3
ROW_LEN = 256
DOC_MOST = 64
GW = 2048
MAXDOC = 8
TOK_DEV = 256
ROWS = 64
TOKENS = 16384
NPAT = 128
N_DP = 64


def doc_layout(key):
    lengths = jax.random.randint(jax.random.fold_in(key, 11), (ROWS, MAXDOC), DOC_MOST // 4, DOC_MOST + 1)
    chosen = jax.random.randint(jax.random.fold_in(key, 12), (ROWS, 1), 0, 2)
    slots = jnp.arange(MAXDOC, dtype=jnp.int32)[None, :]
    lengths = jnp.where(slots == chosen, DOC_MOST, lengths)
    row_ids = jnp.arange(ROWS, dtype=jnp.int32)[:, None]
    lengths = jnp.where(row_ids == 0, DOC_MOST, lengths)
    ends = jnp.cumsum(lengths, axis=1)
    row_count = jnp.max(jnp.where(ends <= ROW_LEN, ends, 0), axis=1)
    starts = jnp.minimum(ends - lengths, row_count[:, None])
    return (starts.astype(jnp.int32), row_count.astype(jnp.int32))


def token_documents(key):
    starts, row_count = doc_layout(key)
    positions = jnp.arange(ROW_LEN, dtype=jnp.int32)
    doc_of = jnp.sum((starts[:, None, :] <= positions[None, :, None]).astype(jnp.int32), axis=2) - 1
    owners = jnp.arange(ROWS, dtype=jnp.int32)[:, None] * MAXDOC + doc_of
    return owners.reshape(TOKENS)


def build_field(key, doc_ids, token_noise, row_scale, feature_count):
    subkeys = jax.random.split(key, 3)
    directions = jax.random.truncated_normal(subkeys[0], -3.0, 3.0, (LAYERS, ROWS * MAXDOC, feature_count))
    shared_part = jnp.take(directions, doc_ids, axis=1)
    feature_scale = jnp.exp(jax.random.uniform(subkeys[2], (LAYERS, 1, feature_count), minval=-1.1512925, maxval=1.1512925)) / 1.4662
    return feature_scale * row_scale * (token_noise + 0.6 * shared_part)


def draw_layer_inputs(key, part):
    doc_ids = token_documents(key)
    key = jax.random.fold_in(key, 21)
    subkeys = jax.random.split(key, 4)
    field_dims = (LAYERS, TOKENS, D)
    token_noise = jax.random.truncated_normal(subkeys[0], -3.0, 3.0, field_dims)
    row_scale = jnp.ones((LAYERS, TOKENS, 1), jnp.float32)
    field_values = build_field(subkeys[2], doc_ids, token_noise, row_scale, D)
    pairing = jax.random.permutation(subkeys[3], N_DP)
    token_block = pairing[jnp.arange(TOKENS, dtype=jnp.int32) // TOK_DEV]
    feature_block = jnp.arange(D, dtype=jnp.int32) // (D // N_DP)
    spike_gain = jnp.where(token_block[:, None] == feature_block[None, :], 2.0, 1.0)
    return jnp.clip(field_values * spike_gain[None, :, :], -8.0, 8.0).astype(jnp.bfloat16)


def draw_layer_outgrads(key, part):
    doc_ids = token_documents(key)
    key = jax.random.fold_in(key, 22)
    subkeys = jax.random.split(key, 3)
    field_dims = (LAYERS, TOKENS, GW)
    token_noise = jax.random.truncated_normal(subkeys[0], -3.0, 3.0, field_dims)
    row_scale = jnp.ones((LAYERS, TOKENS, 1), jnp.float32)
    field_values = build_field(subkeys[2], doc_ids, token_noise, row_scale, GW)
    return jnp.clip(field_values * 0.015625, -0.125, 0.125).astype(jnp.bfloat16)


def draw_doc_starts(key, part):
    starts, row_count = doc_layout(key)
    return starts


def draw_row_tokens(key, part):
    starts, row_count = doc_layout(key)
    return row_count


def plant(entries, rng, least, top_value):
    longest = entries.shape.index(max(entries.shape))
    spots = []
    for shift in (0, 1):
        where = [jax.random.randint(jax.random.fold_in(rng, axis), (), 0, length) for axis, length in enumerate(entries.shape)]
        where[longest] = (where[longest] + shift) % entries.shape[longest]
        spots.append(tuple(where))
    return entries.at[spots[0]].set(least).at[spots[1]].set(top_value)


def setup_inputs(seed: int = 0) -> dict:
    arg_keys = jax.random.split(jax.random.key(seed), 6)
    layer_inputs = draw_layer_inputs(jax.random.fold_in(arg_keys[5], 71), 0)
    layer_outgrads = draw_layer_outgrads(jax.random.fold_in(arg_keys[5], 71), 0)
    doc_starts = draw_doc_starts(jax.random.fold_in(arg_keys[5], 71), 0)
    row_tokens = draw_row_tokens(jax.random.fold_in(arg_keys[5], 71), 0)
    doc_patient = plant(jax.random.randint(arg_keys[4], (ROWS, MAXDOC), 0, NPAT), jax.random.fold_in(arg_keys[4], 1), 0, NPAT - 1).astype(jnp.int32)
    return dict(layer_inputs=layer_inputs, layer_outgrads=layer_outgrads, doc_starts=doc_starts, row_tokens=row_tokens, doc_patient=doc_patient)


def row_layout(starts, row_count, row_len):
    positions = jnp.arange(row_len, dtype=jnp.int32)
    doc_of = lax.optimization_barrier(jnp.sum((starts[None, :] <= positions[:, None]).astype(jnp.int32), axis=1)) - 1
    is_valid = positions < row_count
    slots = jnp.arange(starts.shape[0], dtype=jnp.int32)
    member = ((doc_of[:, None] == slots[None, :]) & is_valid[:, None]).astype(jnp.float32)
    same_doc = ((doc_of[:, None] == doc_of[None, :]) & is_valid[:, None] & is_valid[None, :]).astype(jnp.float32)
    return (member, same_doc)

def gram_of(block):
    return lax.dot_general(block, block, (((1,), (1,)), ((), ())), preferred_element_type=jnp.float32)

def reference(layer_inputs, layer_outgrads, doc_starts, row_tokens, doc_patient):
    clip_bound = DOC_MOST * math.sqrt(LAYERS * D * GW) / 300.0
    row_total = doc_starts.shape[0]
    row_len = layer_inputs.shape[1] // row_total

    def one_row(index):
        first = (index * row_len).astype(jnp.int32)
        inputs_row = lax.dynamic_slice_in_dim(layer_inputs, first, row_len, 1)
        outgrads_row = lax.dynamic_slice_in_dim(layer_outgrads, first, row_len, 1)
        member, same_doc = row_layout(doc_starts[index], row_tokens[index], row_len)
        norms = jnp.zeros((doc_starts.shape[1],), jnp.float32)
        for which_layer in range(LAYERS):
            product = same_doc * gram_of(inputs_row[which_layer]) * gram_of(outgrads_row[which_layer])
            norms = norms + jnp.dot(lax.optimization_barrier(jnp.sum(product, axis=1)), member, precision=lax.Precision.HIGHEST)
        return norms
    doc_norms = lax.map(one_row, jnp.arange(row_total, dtype=jnp.int32))
    next_starts = jnp.concatenate([doc_starts[:, 1:], row_tokens[:, None]], axis=1)
    nonempty = (next_starts > doc_starts).astype(jnp.float32)
    patients = jnp.arange(NPAT, dtype=jnp.int32)
    patient_hits = (doc_patient[:, :, None] == patients[None, None, :]).astype(jnp.float32)
    counts = lax.optimization_barrier(jnp.sum(patient_hits * nonempty[:, :, None], axis=(0, 1)))
    doc_count = lax.optimization_barrier(jnp.sum(patient_hits * counts[None, None, :], axis=2))
    doc_scale = clip_bound / jnp.maximum(clip_bound, jnp.sqrt(doc_norms)) / jnp.maximum(doc_count, 1.0)
    member_all, unused_same = jax.vmap(row_layout, in_axes=(0, 0, None))(doc_starts, row_tokens, row_len)
    token_weight = jnp.einsum('rtd,rd->rt', member_all, doc_scale, precision=lax.Precision.HIGHEST)
    token_weight = token_weight.reshape(row_total * row_len)
    weighted = (token_weight[:, None] * layer_outgrads[0]).astype(jnp.bfloat16)
    weight_grad = lax.dot_general(layer_inputs[0], weighted, (((0,), (0,)), ((), ())), preferred_element_type=jnp.float32)
    return (weight_grad, doc_scale)
```

```python
import functools
import math

import jax
import jax.numpy as jnp
from jax import lax
from jax.experimental import pallas as pl
from jax.experimental.pallas import tpu as pltpu
from jax.sharding import PartitionSpec as P

D = 4096
LAYERS = 3
DOC_MOST = 64
GW = 2048
MAXDOC = 8
TOK = 256
NX = 4
NY = 4
NT = 2 * NX
PIECES = 2
MESH = pl.DeviceIdType.MESH
F32 = jnp.float32
BF16 = jnp.bfloat16


def remote(src, dst, send_sem, recv_sem, device):
    return pltpu.make_async_remote_copy(
        src_ref=src,
        dst_ref=dst,
        send_sem=send_sem,
        recv_sem=recv_sem,
        device_id=device,
        device_id_type=MESH,
    )


def pack_band(gram):
    shape = (64, 128)
    row = lax.broadcasted_iota(jnp.int32, shape, 0)
    lane = lax.broadcasted_iota(jnp.int32, shape, 1)
    upper = lax.rem(lane, 64) >= row
    low_lanes = lane < 64
    halves = []
    for q in range(2):
        base = 128 * q
        first = gram[base : base + 64, base : base + 128]
        second = gram[base + 64 : base + 128, base : base + 128]
        block0 = jnp.where(upper, first, pltpu.roll(first, 64, 1))
        if q == 0:
            across = pltpu.roll(gram[base + 64 : base + 128, base + 128 : base + 256], 64, 1)
        else:
            across = jnp.zeros(shape, F32)
        block1 = jnp.where(upper, second, across)
        halves.append(jnp.where(low_lanes, block0, block1))
    return halves


def gram_of(block):
    return lax.dot_general(block, block, (((1,), (1,)), ((), ())), preferred_element_type=F32)


def kernel(
    nz,
    clip_bound,
    xi_ref,
    g_ref,
    starts_ref,
    rows_ref,
    pat_ref,
    out_ref,
    scale_ref,
    xt,
    xs,
    gy,
    wy,
    gp,
    gr,
    npr,
    hy,
    hz,
    t3,
    part,
    rd,
    ru,
    sc_send,
    sc_recv,
    g_send,
    g_recv,
    hy_send,
    hy_recv,
    hz_send,
    hz_recv,
    gr_send,
    gr_recv,
    np_send,
    np_recv,
    t3_send,
    t3_recv,
    ag_send,
    ag_recv,
    sib_send,
    sib_recv,
    dn_send,
    dn_recv,
    up_send,
    up_recv,
):
    dp = lax.axis_index("dp")
    tensor = lax.axis_index("tensor")
    y = lax.div(dp, nz)
    z = lax.rem(dp, nz)
    x = lax.div(tensor, 2)
    c = lax.rem(tensor, 2)

    def device(yy, zz, xx, cc):
        return (yy * nz + zz, xx * 2 + cc)

    def y_peer(off):
        return device(lax.rem(y + off, NY), z, x, c)

    def z_peer(off):
        return device(y, lax.rem(z + off, nz), x, c)

    def t_peer(off):
        return (dp, lax.rem(tensor + off, NT))

    def x_peer(off):
        return device(y, z, lax.rem(x + off, NX), c)

    sibling = device(y, z, x, 1 - c)
    on_diagonal = x == y

    barrier = pltpu.get_barrier_semaphore()

    def greet(target):
        pl.semaphore_signal(barrier, inc=1, device_id=target, device_id_type=MESH)

    for off in range(1, NT):
        greet(t_peer(off))
    for off in range(1, NY):
        greet(y_peer(off))
    for off in range(1, nz):
        greet(z_peer(off))
    for off in range(1, NX):
        greet(device(x, z, lax.rem(x + off, NX), c))
        greet(device(lax.rem(y + off, NY), z, y, c))

    @pl.when(jnp.logical_not(on_diagonal))
    def _():
        greet(device(x, z, x, c))
        greet(device(y, z, y, c))

    xt[...] = xi_ref[0].T

    starts = [starts_ref[0, d] for d in range(MAXDOC)]
    used = rows_ref[0]
    ends = [jnp.minimum(starts[d + 1], used) if d + 1 < MAXDOC else used for d in range(MAXDOC)]
    patients = [pat_ref[0, d] for d in range(MAXDOC)]
    tile = (8, 128)
    sub8 = lax.broadcasted_iota(jnp.int32, tile, 0)
    lane8 = lax.broadcasted_iota(jnp.int32, tile, 1)
    hist = jnp.zeros(tile, F32)
    patient_of = jnp.zeros(tile, jnp.int32)
    for d in range(MAXDOC):
        nonempty = jnp.where(ends[d] > starts[d], 1.0, 0.0)
        hist = hist + jnp.where(lane8 == patients[d], nonempty, 0.0)
        patient_of = jnp.where(sub8 == d, patients[d], patient_of)
    hy[y] = hist
    gy[y] = g_ref[0]

    pl.semaphore_wait(barrier, NT + NY + nz - 3 + jnp.where(on_diagonal, 2 * (NX - 1), 2 * NX))

    scatter = [
        remote(
            xt.at[pl.ds(pl.multiple_of(lax.rem(x + off, NX) * 128, 128), 128)],
            xs.at[lax.rem(x + off, NX) * 2 + c, y],
            sc_send.at[off],
            sc_recv.at[y],
            device(x, z, lax.rem(x + off, NX), c),
        )
        for off in range(NX)
    ]
    own_piece = pltpu.make_async_copy(
        xt.at[pl.ds(pl.multiple_of(x * 128, 128), 128)], xs.at[tensor, y], sc_recv.at[y]
    )
    for off in range(1, NX):
        scatter[off].start()

    @pl.when(jnp.logical_not(on_diagonal))
    def _():
        scatter[0].start()

    @pl.when(on_diagonal)
    def _():
        own_piece.start()

    hist_y = [
        remote(hy.at[y], hy.at[y], hy_send.at[off], hy_recv.at[off], y_peer(off))
        for off in range(1, NY)
    ]
    for copy in hist_y:
        copy.start()
    outgrads = [
        remote(g_ref.at[0], gy.at[y], g_send.at[off], g_recv.at[off], y_peer(off))
        for off in range(1, NY)
    ]
    for copy in outgrads:
        copy.start()

    for layer in range(LAYERS):
        for which, ref in ((0, xi_ref), (1, g_ref)):
            low, high = pack_band(gram_of(ref[layer]))
            for owner in range(NT):
                source = low if owner < 4 else high
                first = (owner % 4) * 16
                gp[owner, 2 * layer + which] = source[first : first + 16]
    grams = [
        remote(
            gp.at[lax.rem(tensor + off, NT)],
            gr.at[tensor],
            gr_send.at[off],
            gr_recv.at[off],
            t_peer(off),
        )
        for off in range(1, NT)
    ]
    for copy in grams:
        copy.start()

    gathers = []
    for yy in range(NY):
        remote(
            xs.at[tensor, yy], xs.at[tensor, yy], sc_send.at[0], sc_recv.at[yy], sibling
        ).wait_recv()
        block = xs.at[tensor, yy]
        copies = [
            remote(block, block, ag_send.at[0, yy], ag_recv.at[0, yy], x_peer(1)),
            remote(block, block, ag_send.at[1, yy], ag_recv.at[1, yy], x_peer(NX - 1)),
            remote(block, block, sib_send.at[0, yy], sib_recv.at[0, yy], sibling),
        ]
        for copy in copies:
            copy.start()
        gathers += copies

    for off in range(1, NY):
        slot = hy.at[lax.rem(y + NY - off, NY)]
        remote(slot, slot, hy_send.at[off], hy_recv.at[off], y_peer(off)).wait_recv()
    hz[z] = hy[0] + hy[1] + hy[2] + hy[3]
    hist_z = [
        remote(hz.at[z], hz.at[z], hz_send.at[off], hz_recv.at[off], z_peer(off))
        for off in range(1, nz)
    ]
    for copy in hist_z:
        copy.start()

    total = gp[tensor]
    for off in range(1, NT):
        source = lax.rem(tensor + NT - off, NT)
        remote(
            gr.at[source], gr.at[source], gr_send.at[off], gr_recv.at[off], t_peer(off)
        ).wait_recv()
        total = total + gr[source]
    product = total[0] * total[1] + total[2] * total[3] + total[4] * total[5]
    band = (16, 128)
    packed_row = lax.broadcasted_iota(jnp.int32, band, 0) + tensor * 16
    packed_lane = lax.broadcasted_iota(jnp.int32, band, 1)
    inner_row = lax.rem(packed_row, 64)
    inner_lane = lax.rem(packed_lane, 64)
    base = 64 * (2 * lax.div(packed_row, 64) + lax.div(packed_lane, 64))
    tok_t = base + inner_row
    tok_s = base + inner_lane + jnp.where(inner_lane >= inner_row, 0, 64)
    product = product * jnp.where(tok_t == tok_s, 1.0, 2.0)
    norm_part = jnp.zeros(tile, F32)
    for d in range(MAXDOC):
        inside = (
            (tok_t >= starts[d]) & (tok_t < ends[d]) & (tok_s >= starts[d]) & (tok_s < ends[d])
        )
        value = jnp.sum(jnp.where(inside, product, 0.0), keepdims=True)
        norm_part = jnp.where(sub8 == d, value, norm_part)
    npr[tensor] = norm_part
    norms_out = [
        remote(npr.at[tensor], npr.at[tensor], np_send.at[off], np_recv.at[off], t_peer(off))
        for off in range(1, NT)
    ]
    for copy in norms_out:
        copy.start()

    def arrived(hop, yy, source_x, recv_slot):
        slot = xs.at[source_x * 2 + c, yy]
        remote(slot, slot, ag_send.at[hop, yy], recv_slot, sibling).wait_recv()
        return slot

    left_x = lax.rem(x + NX - 1, NX)
    right_x = lax.rem(x + 1, NX)
    far_x = lax.rem(x + 2, NX)
    for yy in range(NY):
        block = arrived(0, yy, left_x, ag_recv.at[0, yy])
        if yy < NY // 2:
            copy = remote(block, block, ag_send.at[2, yy], ag_recv.at[2, yy], x_peer(1))
            copy.start()
            gathers.append(copy)
        copy = remote(block, block, sib_send.at[1, yy], sib_recv.at[1, yy], sibling)
        copy.start()
        gathers.append(copy)
        block = arrived(1, yy, right_x, ag_recv.at[1, yy])
        if yy >= NY // 2:
            copy = remote(block, block, ag_send.at[2, yy], ag_recv.at[2, yy], x_peer(NX - 1))
            copy.start()
            gathers.append(copy)
        copy = remote(block, block, sib_send.at[2, yy], sib_recv.at[2, yy], sibling)
        copy.start()
        gathers.append(copy)

    for off in range(1, nz):
        slot = hz.at[lax.rem(z + nz - off, nz)]
        remote(slot, slot, hz_send.at[off], hz_recv.at[off], z_peer(off)).wait_recv()
    counts = hz[0]
    for zz in range(1, nz):
        counts = counts + hz[zz]
    doc_count = jnp.sum(jnp.where(lane8 == patient_of, counts, 0.0), axis=1, keepdims=True)
    for off in range(1, NT):
        slot = npr.at[lax.rem(tensor + NT - off, NT)]
        remote(slot, slot, np_send.at[off], np_recv.at[off], t_peer(off)).wait_recv()
    norms = npr[0]
    for tt in range(1, NT):
        norms = norms + npr[tt]
    scale = clip_bound / jnp.maximum(clip_bound, jnp.sqrt(norms)) / jnp.maximum(doc_count, 1.0)
    scale_row = jnp.sum(jnp.where(sub8 == lane8, scale, 0.0), axis=0, keepdims=True)
    scale_ref[...] = scale_row[:, :MAXDOC]
    told = jnp.where(sub8 == 2, scale_row, 0.0)
    for d in range(MAXDOC):
        told = jnp.where((sub8 == 0) & (lane8 == d), starts[d].astype(F32), told)
        told = jnp.where((sub8 == 1) & (lane8 == d), ends[d].astype(F32), told)
    t3[y] = told
    told_out = [
        remote(t3.at[y], t3.at[y], t3_send.at[off], t3_recv.at[off], y_peer(off))
        for off in range(1, NY)
    ]
    for copy in told_out:
        copy.start()

    for yy in range(NY):
        block = arrived(2, yy, far_x, ag_recv.at[2, yy])
        copy = remote(block, block, sib_send.at[3, yy], sib_recv.at[3, yy], sibling)
        copy.start()
        gathers.append(copy)

    for off in range(1, NY):
        source = lax.rem(y + NY - off, NY)
        slot = gy.at[source]
        remote(slot, slot, g_send.at[off], g_recv.at[off], y_peer(off)).wait_recv()
        slot = t3.at[source]
        remote(slot, slot, t3_send.at[off], t3_recv.at[off], y_peer(off)).wait_recv()
    token = lax.broadcasted_iota(jnp.int32, (TOK, 128), 0).astype(F32)
    for yy in range(NY):
        inside = (token >= t3[yy, 0:1, :]) & (token < t3[yy, 1:2, :])
        weight = jnp.sum(jnp.where(inside, t3[yy, 2:3, :], 0.0), axis=1, keepdims=True)
        wy[yy] = (weight * gy[yy].astype(F32)).astype(BF16)

    for hop, source_x in enumerate((x, left_x, right_x, far_x)):
        for yy in range(NY):
            slot = xs.at[source_x * 2 + 1 - c, yy]
            remote(slot, slot, sib_send.at[hop, yy], sib_recv.at[hop, yy], sibling).wait_recv()

    for tt in range(NT):
        sums = jnp.dot(xs[tt, 0], wy[0], preferred_element_type=F32)
        for yy in range(1, NY):
            sums = sums + jnp.dot(xs[tt, yy], wy[yy], preferred_element_type=F32)
        owner = 8 * (tt % 2) + 2 * (tt // 2)
        part[owner] = sums[:64]
        part[owner + 1] = sums[64:]

    below, above = z_peer(nz - 1), z_peer(1)
    half = nz // 2
    rows = 64 // PIECES
    chain = []

    def step(s, owner, arrivals, send, recv, target):
        for j in range(PIECES):
            span = pl.ds(j * rows, rows)
            mine = part.at[owner, span]
            if s > 0:
                slot = arrivals.at[s - 1, span]
                remote(slot, slot, send.at[s - 1, j], recv.at[s - 1, j], target).wait_recv()
                mine[...] += slot[...]
            copy = remote(mine, arrivals.at[s, span], send.at[s, j], recv.at[s, j], target)
            copy.start()
            chain.append(copy)

    for s in range(half):
        step(s, lax.rem(z + nz - half + s, nz), rd, dn_send, dn_recv, below)
        if s < half - 1:
            step(s, lax.rem(z + half - 1 - s, nz), ru, up_send, up_recv, above)
    for j in range(PIECES):
        span = pl.ds(j * rows, rows)
        last_up = ru.at[half - 2, span]
        remote(
            last_up, last_up, up_send.at[half - 2, j], up_recv.at[half - 2, j], above
        ).wait_recv()
        last_down = rd.at[half - 1, span]
        remote(
            last_down, last_down, dn_send.at[half - 1, j], dn_recv.at[half - 1, j], below
        ).wait_recv()
        out_ref[span, :] = part[z, span, :] + last_up[...] + last_down[...]

    for off in range(1, NX):
        scatter[off].wait_send()

    @pl.when(jnp.logical_not(on_diagonal))
    def _():
        scatter[0].wait_send()

    for copy in hist_y + outgrads + grams + gathers + hist_z + norms_out + told_out + chain:
        copy.wait_send()


def on_device(nz, layer_inputs, layer_outgrads, doc_starts, row_tokens, doc_patient):
    clip_bound = DOC_MOST * math.sqrt(LAYERS * D * GW) / 300.0
    half = nz // 2
    vmem = pl.BlockSpec(memory_space=pltpu.VMEM)
    smem = pl.BlockSpec(memory_space=pltpu.SMEM)
    dma = pltpu.SemaphoreType.DMA
    return pl.pallas_call(
        functools.partial(kernel, nz, clip_bound),
        out_shape=(
            jax.ShapeDtypeStruct((64, 256), F32),
            jax.ShapeDtypeStruct((1, MAXDOC), F32),
        ),
        in_specs=[vmem, vmem, smem, smem, smem],
        out_specs=(vmem, vmem),
        scratch_shapes=[
            pltpu.VMEM((512, TOK), BF16),
            pltpu.VMEM((NT, NY, 128, TOK), BF16),
            pltpu.VMEM((NY, TOK, 256), BF16),
            pltpu.VMEM((NY, TOK, 256), BF16),
            pltpu.VMEM((NT, 6, 16, 128), F32),
            pltpu.VMEM((NT, 6, 16, 128), F32),
            pltpu.VMEM((NT, 8, 128), F32),
            pltpu.VMEM((NY, 8, 128), F32),
            pltpu.VMEM((nz, 8, 128), F32),
            pltpu.VMEM((NY, 8, 128), F32),
            pltpu.VMEM((nz, 64, 256), F32),
            pltpu.VMEM((half, 64, 256), F32),
            pltpu.VMEM((half - 1, 64, 256), F32),
            dma((NX,)),
            dma((NY,)),
            dma((NY,)),
            dma((NY,)),
            dma((NY,)),
            dma((NY,)),
            dma((nz,)),
            dma((nz,)),
            dma((NT,)),
            dma((NT,)),
            dma((NT,)),
            dma((NT,)),
            dma((NY,)),
            dma((NY,)),
            dma((3, NY)),
            dma((3, NY)),
            dma((4, NY)),
            dma((4, NY)),
            dma((half, PIECES)),
            dma((half, PIECES)),
            dma((half - 1, PIECES)),
            dma((half - 1, PIECES)),
        ],
        compiler_params=pltpu.CompilerParams(
            collective_id=0, has_side_effects=True, vmem_limit_bytes=40 * 1024 * 1024
        ),
    )(layer_inputs, layer_outgrads, doc_starts, row_tokens, doc_patient)


def solution(mesh):
    placed = (
        P(None, "dp", "tensor"),
        P(None, "dp", "tensor"),
        P("dp", None),
        P("dp"),
        P("dp", None),
    )
    return jax.shard_map(
        functools.partial(on_device, mesh.shape["dp"] // NY),
        mesh=mesh,
        in_specs=placed,
        out_specs=(P("dp", "tensor"), P("dp", None)),
        check_vma=False,
    )
```

```python
import functools
import math

import jax
import jax.numpy as jnp
from jax import lax
from jax.experimental import pallas as pl
from jax.experimental.pallas import tpu as pltpu
from jax.sharding import PartitionSpec as P

D = 4096
LAYERS = 3
DOC_MOST = 64
GW = 2048
MAXDOC = 8
TOK = 256
NX = 4
NY = 4
NT = 2 * NX
WINDOW = (0, 1, -1, 2)
NW = len(WINDOW)
PIECE = 128 // NW
BLOCKS = 4
PIECES = 2
GRAM_TYPE = jnp.float32
MESH = pl.DeviceIdType.MESH
F32 = jnp.float32
BF16 = jnp.bfloat16


def remote(src, dst, send_sem, recv_sem, device):
    return pltpu.make_async_remote_copy(
        src_ref=src,
        dst_ref=dst,
        send_sem=send_sem,
        recv_sem=recv_sem,
        device_id=device,
        device_id_type=MESH,
    )


def pack_band(gram):
    shape = (64, 128)
    row = lax.broadcasted_iota(jnp.int32, shape, 0)
    lane = lax.broadcasted_iota(jnp.int32, shape, 1)
    upper = lax.rem(lane, 64) >= row
    low_lanes = lane < 64
    halves = []
    for q in range(2):
        base = 128 * q
        first = gram[base : base + 64, base : base + 128]
        second = gram[base + 64 : base + 128, base : base + 128]
        block0 = jnp.where(upper, first, pltpu.roll(first, 64, 1))
        if q == 0:
            across = pltpu.roll(gram[base + 64 : base + 128, base + 128 : base + 256], 64, 1)
        else:
            across = jnp.zeros(shape, F32)
        block1 = jnp.where(upper, second, across)
        halves.append(jnp.where(low_lanes, block0, block1))
    return halves


def gram_of(block):
    return lax.dot_general(block, block, (((1,), (1,)), ((), ())), preferred_element_type=F32)


def kernel(
    nz,
    clip_bound,
    xi_ref,
    g_ref,
    starts_in,
    rows_in,
    pat_in,
    out_ref,
    scale_ref,
    starts_ref,
    rows_ref,
    pat_ref,
    xv,
    gv,
    xt,
    xs,
    gy,
    wy,
    gp,
    gr,
    npr,
    hist,
    ring,
    told,
    part,
    rd,
    ru,
    in_sem,
    sc_send,
    sc_recv,
    gz_send,
    gz_recv,
    gy_send,
    gy_recv,
    gf_send,
    gf_recv,
    hist_send,
    hist_recv,
    ring_send,
    ring_recv,
    gr_send,
    gr_recv,
    np_send,
    np_recv,
    told_send,
    told_recv,
    ag_send,
    ag_recv,
    sib_send,
    sib_recv,
    dn_send,
    dn_recv,
    up_send,
    up_recv,
):
    dp = lax.axis_index("dp")
    tensor = lax.axis_index("tensor")
    y = lax.div(dp, nz)
    z = lax.rem(dp, nz)
    x = lax.div(tensor, 2)
    c = lax.rem(tensor, 2)
    members = nz // NW
    place = lax.div(z, NW)

    def device(yy, zz, xx, cc):
        return (yy * nz + zz, xx * 2 + cc)

    def z_at(off):
        return lax.rem(z + off + nz, nz)

    def y_at(off):
        return lax.rem(y + off + NY, NY)

    def x_at(off):
        return lax.rem(x + off + NX, NX)

    def t_at(off):
        return lax.rem(tensor + off + NT, NT)

    def x_peer(off):
        return device(y, z, x_at(off), c)

    def y_peer(off):
        return device(y_at(off), z, x, c)

    sibling = device(y, z, x, 1 - c)
    below, above = device(y, z_at(-NW), x, c), device(y, z_at(NW), x, c)
    on_diagonal = x == y
    window_pairs = [(wi, off) for wi in range(NW) for off in range(NY) if (wi, off) != (0, 0)]
    piece_pairs = [(wi, off) for wi in range(NW) for off in range(NX) if (wi, off) != (0, 0)]

    barrier = pltpu.get_barrier_semaphore()

    def greet(target):
        pl.semaphore_signal(barrier, inc=1, device_id=target, device_id_type=MESH)

    for off in range(1, NT):
        greet((dp, t_at(off)))
    for wi, off in window_pairs:
        greet(device(y_at(off), z_at(-WINDOW[wi]), x, c))
        greet(device(y_at(-off), z_at(WINDOW[wi]), x, c))
    for wi, off in piece_pairs:
        greet(device(x, z_at(-WINDOW[wi]), x_at(off), c))
        greet(device(y_at(off), z_at(WINDOW[wi]), y, c))
    greet(below)
    greet(above)

    @pl.when(jnp.logical_not(on_diagonal))
    def _():
        greet(device(x, z, x, c))
        greet(device(y, z, y, c))

    greetings = NT - 1 + 2 * len(window_pairs) + 2 * len(piece_pairs) + 2

    own_grads = gy.at[0, y]
    loads = [
        pltpu.make_async_copy(xi_ref.at[0], xv.at[0], in_sem.at[0]),
        pltpu.make_async_copy(g_ref.at[0], own_grads, in_sem.at[1]),
        pltpu.make_async_copy(starts_in, starts_ref, in_sem.at[2]),
        pltpu.make_async_copy(rows_in, rows_ref, in_sem.at[3]),
        pltpu.make_async_copy(pat_in, pat_ref, in_sem.at[4]),
        pltpu.make_async_copy(xi_ref.at[pl.ds(1, 2)], xv.at[pl.ds(1, 2)], in_sem.at[5]),
        pltpu.make_async_copy(g_ref.at[pl.ds(1, 2)], gv, in_sem.at[6]),
    ]
    for copy in loads:
        copy.start()

    for copy in loads[2:5]:
        copy.wait()
    starts = [starts_ref[0, d] for d in range(MAXDOC)]
    used = rows_ref[0]
    ends = [jnp.minimum(starts[d + 1], used) if d + 1 < MAXDOC else used for d in range(MAXDOC)]
    patients = [pat_ref[0, d] for d in range(MAXDOC)]
    tile = (8, 128)
    sub8 = lax.broadcasted_iota(jnp.int32, tile, 0)
    lane8 = lax.broadcasted_iota(jnp.int32, tile, 1)
    own_hist = jnp.zeros(tile, F32)
    patient_of = jnp.zeros(tile, jnp.int32)
    for d in range(MAXDOC):
        nonempty = jnp.where(ends[d] > starts[d], 1.0, 0.0)
        own_hist = own_hist + jnp.where(lane8 == patients[d], nonempty, 0.0)
        patient_of = jnp.where(sub8 == d, patients[d], patient_of)
    hist[0, y] = own_hist

    def put_gram(which, block):
        low, high = pack_band(gram_of(block))
        for owner in range(NT):
            source = low if owner < 4 else high
            first = (owner % 4) * 16
            gp[owner, which] = source[first : first + 16].astype(GRAM_TYPE)

    loads[0].wait()
    xt[...] = xv[0].T
    put_gram(0, xv[0])
    loads[1].wait()
    put_gram(1, gy[0, y])
    loads[5].wait()
    loads[6].wait()
    for layer in range(1, LAYERS):
        put_gram(2 * layer, xv[layer])
        put_gram(2 * layer + 1, gv[layer - 1])

    pl.semaphore_wait(barrier, greetings + jnp.where(on_diagonal, 0, 2))

    sent = []

    def send(src, dst, send_sem, recv_sem, target):
        copy = remote(src, dst, send_sem, recv_sem, target)
        copy.start()
        sent.append(copy)

    def wait_for(slot, send_sem, recv_sem):
        remote(slot, slot, send_sem, recv_sem, sibling).wait_recv()

    for off in range(1, NT):
        send(gp.at[t_at(off)], gr.at[tensor], gr_send.at[off], gr_recv.at[off], (dp, t_at(off)))

    def to_window(ref, send_sem, recv_sem):
        for wi, off in window_pairs:
            send(
                ref.at[0, y],
                ref.at[wi, y],
                send_sem.at[wi, off],
                recv_sem.at[wi, off],
                device(y_at(off), z_at(-WINDOW[wi]), x, c),
            )

    def from_window(ref, send_sem, recv_sem):
        for wi, off in window_pairs:
            wait_for(ref.at[wi, y_at(-off)], send_sem.at[wi, off], recv_sem.at[wi, off])

    to_window(hist, hist_send, hist_recv)

    def piece(wi, off):
        k = x_at(off)
        kind = lax.rem(z_at(-WINDOW[wi]), NW)
        first = k * PIECE
        row = 64 * (kind + NW * lax.div(first, 64)) + lax.rem(first, 64)
        return xt.at[pl.ds(pl.multiple_of(row, PIECE), PIECE)]

    def scatter(wi, off):
        k = x_at(off)
        return remote(
            piece(wi, off),
            xs.at[wi, y, k * 2 + c],
            sc_send.at[wi, off],
            sc_recv.at[wi, y],
            device(x, z_at(-WINDOW[wi]), k, c),
        )

    own_piece = pltpu.make_async_copy(piece(0, 0), xs.at[0, y, tensor], sc_recv.at[0, y])
    own_scatter = scatter(0, 0)

    @pl.when(jnp.logical_not(on_diagonal))
    def _():
        own_scatter.start()

    @pl.when(on_diagonal)
    def _():
        own_piece.start()

    for wi, off in piece_pairs:
        copy = scatter(wi, off)
        copy.start()
        sent.append(copy)

    for wi in range(1, NW):
        send(
            own_grads,
            gy.at[wi, y],
            gz_send.at[wi],
            gz_recv.at[wi],
            device(y, z_at(-WINDOW[wi]), x, c),
        )

    def grads_along_y(wi):
        block = gy.at[wi, y]
        send(block, block, gy_send.at[wi, 0], gy_recv.at[wi, 0], y_peer(1))
        send(block, block, gy_send.at[wi, 1], gy_recv.at[wi, 1], y_peer(-1))

    def grads_onward(wi):
        for way, step in ((0, 1), (1, -1)):
            block = gy.at[wi, y_at(-step)]
            wait_for(block, gy_send.at[wi, way], gy_recv.at[wi, way])
            half = gy.at[wi, y_at(-step), pl.ds(128 * way, 128)]
            send(half, half, gf_send.at[wi, way], gf_recv.at[wi, way], y_peer(step))

    grads_along_y(0)

    span = NW * NY // BLOCKS
    blocks = [(b * span // NY, b * span % NY) for b in range(BLOCKS)]

    def block_of(b, source_x, source_c):
        wi, first = blocks[b]
        return xs.at[wi, pl.ds(first, span), source_x * 2 + source_c]

    for b in range(BLOCKS):
        wi, first = blocks[b]
        for yy in range(first, first + span):
            wait_for(xs.at[wi, yy, tensor], sc_send.at[0, 0], sc_recv.at[wi, yy])
        block = block_of(b, x, c)
        send(block, block, ag_send.at[0, b], ag_recv.at[0, b], x_peer(1))
        send(block, block, ag_send.at[1, b], ag_recv.at[1, b], x_peer(-1))
        send(block, block, sib_send.at[0, b], sib_recv.at[0, b], sibling)

    from_window(hist, hist_send, hist_recv)
    window_count = hist[0, 0]
    for wi in range(NW):
        for yy in range(NY):
            if (wi, yy) != (0, 0):
                window_count = window_count + hist[wi, yy]
    ring[place] = window_count
    half_ring = members // 2

    def ring_send_step(s):
        down = ring.at[lax.rem(place + s, members)]
        send(down, down, ring_send.at[0, s], ring_recv.at[0, s], below)
        if s < members - 1 - half_ring:
            up = ring.at[lax.rem(place + members - s, members)]
            send(up, up, ring_send.at[1, s], ring_recv.at[1, s], above)

    def ring_wait_step(s):
        down = ring.at[lax.rem(place + s + 1, members)]
        wait_for(down, ring_send.at[0, s], ring_recv.at[0, s])
        if s < members - 1 - half_ring:
            up = ring.at[lax.rem(place + members - s - 1, members)]
            wait_for(up, ring_send.at[1, s], ring_recv.at[1, s])

    ring_send_step(0)
    grads_onward(0)

    total = gp[tensor].astype(F32)
    for off in range(1, NT):
        source = t_at(-off)
        wait_for(gr.at[source], gr_send.at[off], gr_recv.at[off])
        total = total + gr[source].astype(F32)
    product = total[0] * total[1] + total[2] * total[3] + total[4] * total[5]
    band = (16, 128)
    packed_row = lax.broadcasted_iota(jnp.int32, band, 0) + tensor * 16
    packed_lane = lax.broadcasted_iota(jnp.int32, band, 1)
    inner_row = lax.rem(packed_row, 64)
    inner_lane = lax.rem(packed_lane, 64)
    base = 64 * (2 * lax.div(packed_row, 64) + lax.div(packed_lane, 64))
    tok_t = base + inner_row
    tok_s = base + inner_lane + jnp.where(inner_lane >= inner_row, 0, 64)
    product = product * jnp.where(tok_t == tok_s, 1.0, 2.0)
    norm_part = jnp.zeros(tile, F32)
    for d in range(MAXDOC):
        inside = (
            (tok_t >= starts[d]) & (tok_t < ends[d]) & (tok_s >= starts[d]) & (tok_s < ends[d])
        )
        value = jnp.sum(jnp.where(inside, product, 0.0), keepdims=True)
        norm_part = jnp.where(sub8 == d, value, norm_part)
    npr[tensor] = norm_part
    for off in range(1, NT):
        send(
            npr.at[tensor], npr.at[tensor], np_send.at[off], np_recv.at[off], (dp, t_at(off))
        )

    for wi in range(1, NW):
        wait_for(gy.at[wi, y], gz_send.at[wi], gz_recv.at[wi])
        grads_along_y(wi)

    for b in range(BLOCKS):
        for hop, step in ((0, 1), (1, -1)):
            block = block_of(b, x_at(-step), c)
            wait_for(block, ag_send.at[hop, b], ag_recv.at[hop, b])
            if (b < BLOCKS // 2) == (hop == 0):
                send(block, block, ag_send.at[2, b], ag_recv.at[2, b], x_peer(step))
            send(block, block, sib_send.at[hop + 1, b], sib_recv.at[hop + 1, b], sibling)

    for s in range(half_ring):
        ring_wait_step(s)
        if s + 1 < half_ring:
            ring_send_step(s + 1)
    counts = ring[0]
    for m in range(1, members):
        counts = counts + ring[m]
    doc_count = jnp.sum(jnp.where(lane8 == patient_of, counts, 0.0), axis=1, keepdims=True)
    for off in range(1, NT):
        wait_for(npr.at[t_at(-off)], np_send.at[off], np_recv.at[off])
    norms = npr[0]
    for tt in range(1, NT):
        norms = norms + npr[tt]
    scale = clip_bound / jnp.maximum(clip_bound, jnp.sqrt(norms)) / jnp.maximum(doc_count, 1.0)
    position = lane8 + 128 * sub8
    weights = jnp.zeros(tile, F32)
    for d in range(MAXDOC):
        weights = jnp.where(
            (position >= starts[d]) & (position < ends[d]), scale[d : d + 1, :], weights
        )
    told[0, y] = weights
    to_window(told, told_send, told_recv)
    scale_row = jnp.sum(jnp.where(sub8 == lane8, scale, 0.0), axis=0, keepdims=True)
    scale_ref[...] = scale_row[:, :MAXDOC]

    for wi in range(1, NW):
        grads_onward(wi)

    for b in range(BLOCKS):
        block = block_of(b, x_at(2), c)
        wait_for(block, ag_send.at[2, b], ag_recv.at[2, b])
        send(block, block, sib_send.at[3, b], sib_recv.at[3, b], sibling)

    from_window(told, told_send, told_recv)
    columns = told[...].reshape(NW * NY * 8, 128).T
    for wi in range(NW):
        for way in range(2):
            half = gy.at[wi, y_at(2), pl.ds(128 * way, 128)]
            wait_for(half, gf_send.at[wi, way], gf_recv.at[wi, way])
        for yy in range(NY):
            for way in range(2):
                lane = (wi * NY + yy) * 8 + way
                rows = pl.ds(128 * way, 128)
                weight = columns[:, lane : lane + 1]
                wy[wi, yy, rows] = (weight * gy[wi, yy, rows].astype(F32)).astype(BF16)

    for hop, source_x in enumerate((x, x_at(-1), x_at(1), x_at(2))):
        for b in range(BLOCKS):
            wait_for(block_of(b, source_x, 1 - c), sib_send.at[hop, b], sib_recv.at[hop, b])

    sums = None
    for wi in range(NW):
        for yy in range(NY):
            features = xs[wi, yy].reshape(NT * PIECE, TOK)
            term = jnp.dot(features, wy[wi, yy], preferred_element_type=F32)
            sums = term if sums is None else sums + term
    step_rows = min(PIECE, 64)
    for tt in range(NT):
        for q in range(0, PIECE, step_rows):
            inner = (tt // 2) * PIECE + q
            owner = (tt % 2) * (8 // NW) + inner // 64
            first = tt * PIECE + q
            part[owner, inner % 64 : inner % 64 + step_rows] = sums[first : first + step_rows]

    rows = 64 // PIECES

    def down_steps(j):
        return half_ring - j % 2

    def chain_step(s, j, owner, arrivals, send_sem, recv_sem, target):
        at = pl.ds(j * rows, rows)
        mine = part.at[owner, at]
        if s > 0:
            slot = arrivals.at[s - 1, at]
            wait_for(slot, send_sem.at[s - 1, j], recv_sem.at[s - 1, j])
            mine[...] += slot[...]
        send(mine, arrivals.at[s, at], send_sem.at[s, j], recv_sem.at[s, j], target)

    for s in range(half_ring):
        for j in range(PIECES):
            down = down_steps(j)
            up = members - 1 - down
            if s < down:
                owner = lax.rem(place + members - down + s, members)
                chain_step(s, j, owner, rd, dn_send, dn_recv, below)
            if s < up:
                owner = lax.rem(place + up - s, members)
                chain_step(s, j, owner, ru, up_send, up_recv, above)
    for j in range(PIECES):
        at = pl.ds(j * rows, rows)
        down = down_steps(j)
        up = members - 1 - down
        value = part[place, at, :]
        if down > 0:
            slot = rd.at[down - 1, at]
            wait_for(slot, dn_send.at[down - 1, j], dn_recv.at[down - 1, j])
            value = value + slot[...]
        if up > 0:
            slot = ru.at[up - 1, at]
            wait_for(slot, up_send.at[up - 1, j], up_recv.at[up - 1, j])
            value = value + slot[...]
        out_ref[at, :] = value

    @pl.when(jnp.logical_not(on_diagonal))
    def _():
        own_scatter.wait_send()

    for copy in sent:
        copy.wait_send()


def on_device(nz, layer_inputs, layer_outgrads, doc_starts, row_tokens, doc_patient):
    clip_bound = DOC_MOST * math.sqrt(LAYERS * D * GW) / 300.0
    members = nz // NW
    half = members // 2
    vmem = pl.BlockSpec(memory_space=pltpu.VMEM)
    anywhere = pl.BlockSpec(memory_space=pl.ANY)
    dma = pltpu.SemaphoreType.DMA
    return pl.pallas_call(
        functools.partial(kernel, nz, clip_bound),
        out_shape=(
            jax.ShapeDtypeStruct((64, 256), F32),
            jax.ShapeDtypeStruct((1, MAXDOC), F32),
        ),
        in_specs=[anywhere] * 5,
        out_specs=(vmem, vmem),
        scratch_shapes=[
            pltpu.SMEM((1, MAXDOC), jnp.int32),
            pltpu.SMEM((1,), jnp.int32),
            pltpu.SMEM((1, MAXDOC), jnp.int32),
            pltpu.VMEM((LAYERS, TOK, 512), BF16),
            pltpu.VMEM((LAYERS - 1, TOK, 256), BF16),
            pltpu.VMEM((512, TOK), BF16),
            pltpu.VMEM((NW, NY, NT, PIECE, TOK), BF16),
            pltpu.VMEM((NW, NY, TOK, 256), BF16),
            pltpu.VMEM((NW, NY, TOK, 256), BF16),
            pltpu.VMEM((NT, 6, 16, 128), GRAM_TYPE),
            pltpu.VMEM((NT, 6, 16, 128), GRAM_TYPE),
            pltpu.VMEM((NT, 8, 128), F32),
            pltpu.VMEM((NW, NY, 8, 128), F32),
            pltpu.VMEM((members, 8, 128), F32),
            pltpu.VMEM((NW, NY, 8, 128), F32),
            pltpu.VMEM((members, 64, 256), F32),
            pltpu.VMEM((half, 64, 256), F32),
            pltpu.VMEM((half, 64, 256), F32),
            dma((7,)),
            dma((NW, NX)),
            dma((NW, NY)),
            dma((NW,)),
            dma((NW,)),
            dma((NW, 2)),
            dma((NW, 2)),
            dma((NW, 2)),
            dma((NW, 2)),
            dma((NW, NY)),
            dma((NW, NY)),
            dma((2, half)),
            dma((2, half)),
            dma((NT,)),
            dma((NT,)),
            dma((NT,)),
            dma((NT,)),
            dma((NW, NY)),
            dma((NW, NY)),
            dma((3, BLOCKS)),
            dma((3, BLOCKS)),
            dma((4, BLOCKS)),
            dma((4, BLOCKS)),
            dma((half, PIECES)),
            dma((half, PIECES)),
            dma((half, PIECES)),
            dma((half, PIECES)),
        ],
        compiler_params=pltpu.CompilerParams(
            collective_id=0, has_side_effects=True, vmem_limit_bytes=40 * 1024 * 1024
        ),
    )(layer_inputs, layer_outgrads, doc_starts, row_tokens, doc_patient)


def solution(mesh):
    placed = (
        P(None, "dp", "tensor"),
        P(None, "dp", "tensor"),
        P("dp", None),
        P("dp"),
        P("dp", None),
    )
    return jax.shard_map(
        functools.partial(on_device, mesh.shape["dp"] // NY),
        mesh=mesh,
        in_specs=placed,
        out_specs=(P("dp", "tensor"), P("dp", None)),
        check_vma=False,
    )
```

```python
import functools
import math

import jax
import jax.numpy as jnp
from jax import lax
from jax.experimental import pallas as pl
from jax.experimental.pallas import tpu as pltpu
from jax.sharding import PartitionSpec as P

D = 4096
LAYERS = 3
DOC_MOST = 64
GW = 2048
MAXDOC = 8
TOK = 256
NX = 4
NY = 4
NT = 2 * NX
WINDOW = (0, 1)
NW = len(WINDOW)
PIECE = 128 // NW
BLOCKS = 4
PIECES = 2
VMEM_BYTES = 63283200
GRAM_TYPE = jnp.bfloat16
MESH = pl.DeviceIdType.MESH
F32 = jnp.float32
BF16 = jnp.bfloat16


def remote(src, dst, send_sem, recv_sem, device):
    return pltpu.make_async_remote_copy(
        src_ref=src,
        dst_ref=dst,
        send_sem=send_sem,
        recv_sem=recv_sem,
        device_id=device,
        device_id_type=MESH,
    )


def pack_band(gram):
    shape = (64, 128)
    row = lax.broadcasted_iota(jnp.int32, shape, 0)
    lane = lax.broadcasted_iota(jnp.int32, shape, 1)
    upper = lax.rem(lane, 64) >= row
    low_lanes = lane < 64
    halves = []
    for q in range(2):
        base = 128 * q
        first = gram[base : base + 64, base : base + 128]
        second = gram[base + 64 : base + 128, base : base + 128]
        block0 = jnp.where(upper, first, pltpu.roll(first, 64, 1))
        if q == 0:
            across = pltpu.roll(gram[base + 64 : base + 128, base + 128 : base + 256], 64, 1)
        else:
            across = jnp.zeros(shape, F32)
        block1 = jnp.where(upper, second, across)
        halves.append(jnp.where(low_lanes, block0, block1))
    return halves


def gram_of(block):
    return lax.dot_general(block, block, (((1,), (1,)), ((), ())), preferred_element_type=F32)


def kernel(
    nz,
    clip_bound,
    xi_ref,
    g_ref,
    starts_in,
    rows_in,
    pat_in,
    out_ref,
    scale_ref,
    starts_ref,
    rows_ref,
    pat_ref,
    xv,
    gv,
    xt,
    xs,
    gy,
    wy,
    gp,
    gr,
    npr,
    hist,
    ring,
    told,
    part,
    sums_in,
    in_sem,
    sc_send,
    sc_recv,
    gz_send,
    gz_recv,
    gy_send,
    gy_recv,
    gf_send,
    gf_recv,
    hist_send,
    hist_recv,
    ring_send,
    ring_recv,
    gr_send,
    gr_recv,
    np_send,
    np_recv,
    told_send,
    told_recv,
    ag_send,
    ag_recv,
    sib_send,
    sib_recv,
    sum_sent,
    sum_recv,
):
    dp = lax.axis_index("dp")
    tensor = lax.axis_index("tensor")
    y = lax.div(dp, nz)
    z = lax.rem(dp, nz)
    x = lax.div(tensor, 2)
    c = lax.rem(tensor, 2)
    members = 8
    place = lax.div(z, NW)

    def device(yy, zz, xx, cc):
        return (yy * nz + zz, xx * 2 + cc)

    def z_at(off):
        return lax.rem(z + off + nz, nz)

    def y_at(off):
        return lax.rem(y + off + NY, NY)

    def x_at(off):
        return lax.rem(x + off + NX, NX)

    def t_at(off):
        return lax.rem(tensor + off + NT, NT)

    def x_peer(off):
        return device(y, z, x_at(off), c)

    def y_peer(off):
        return device(y_at(off), z, x, c)

    sibling = device(y, z, x, 1 - c)
    below, above = device(y, z_at(-NW), x, c), device(y, z_at(NW), x, c)
    below2, above2 = device(y, z_at(-2 * NW), x, c), device(y, z_at(2 * NW), x, c)
    on_diagonal = x == y
    window_pairs = [(wi, off) for wi in range(NW) for off in range(NY) if (wi, off) != (0, 0)]
    piece_pairs = [(wi, off) for wi in range(NW) for off in range(NX) if (wi, off) != (0, 0)]

    barrier = pltpu.get_barrier_semaphore()

    def greet(target):
        pl.semaphore_signal(barrier, inc=1, device_id=target, device_id_type=MESH)

    for off in range(1, NT):
        greet((dp, t_at(off)))
    window_peers = {(off, way * d) for d in WINDOW for way in (1, -1) for off in range(NY)}
    window_peers = sorted(window_peers - {(0, 0)})
    for off, d in window_peers:
        greet(device(y_at(off), z_at(d), x, c))
    for wi, off in piece_pairs:
        greet(device(x, z_at(-WINDOW[wi]), x_at(off), c))
        greet(device(y_at(off), z_at(WINDOW[wi]), y, c))
    for target in (below, above, below2, above2):
        greet(target)

    @pl.when(jnp.logical_not(on_diagonal))
    def _():
        greet(device(x, z, x, c))
        greet(device(y, z, y, c))

    greetings = NT - 1 + len(window_peers) + 2 * len(piece_pairs) + 4

    own_grads = gy.at[0, y]
    loads = [
        pltpu.make_async_copy(xi_ref.at[0], xv.at[0], in_sem.at[0]),
        pltpu.make_async_copy(g_ref.at[0], own_grads, in_sem.at[1]),
        pltpu.make_async_copy(starts_in, starts_ref, in_sem.at[2]),
        pltpu.make_async_copy(rows_in, rows_ref, in_sem.at[3]),
        pltpu.make_async_copy(pat_in, pat_ref, in_sem.at[4]),
        pltpu.make_async_copy(xi_ref.at[pl.ds(1, 2)], xv.at[pl.ds(1, 2)], in_sem.at[5]),
        pltpu.make_async_copy(g_ref.at[pl.ds(1, 2)], gv, in_sem.at[6]),
    ]
    for copy in loads:
        copy.start()

    for copy in loads[2:5]:
        copy.wait()
    starts = [starts_ref[0, d] for d in range(MAXDOC)]
    used = rows_ref[0]
    ends = [jnp.minimum(starts[d + 1], used) if d + 1 < MAXDOC else used for d in range(MAXDOC)]
    patients = [pat_ref[0, d] for d in range(MAXDOC)]
    tile = (8, 128)
    sub8 = lax.broadcasted_iota(jnp.int32, tile, 0)
    lane8 = lax.broadcasted_iota(jnp.int32, tile, 1)
    own_hist = jnp.zeros(tile, F32)
    patient_of = jnp.zeros(tile, jnp.int32)
    for d in range(MAXDOC):
        nonempty = jnp.where(ends[d] > starts[d], 1.0, 0.0)
        own_hist = own_hist + jnp.where(lane8 == patients[d], nonempty, 0.0)
        patient_of = jnp.where(sub8 == d, patients[d], patient_of)
    hist[0, y] = own_hist

    def put_gram(which, block):
        low, high = pack_band(gram_of(block))
        for owner in range(NT):
            source = low if owner < 4 else high
            first = (owner % 4) * 16
            gp[owner, which] = source[first : first + 16].astype(GRAM_TYPE)

    loads[0].wait()
    xt[...] = xv[0].T
    put_gram(0, xv[0])
    loads[1].wait()
    put_gram(1, gy[0, y])
    loads[5].wait()
    loads[6].wait()
    for layer in range(1, LAYERS):
        put_gram(2 * layer, xv[layer])
        put_gram(2 * layer + 1, gv[layer - 1])

    pl.semaphore_wait(barrier, greetings + jnp.where(on_diagonal, 0, 2))

    sent = []

    def send(src, dst, send_sem, recv_sem, target):
        copy = remote(src, dst, send_sem, recv_sem, target)
        copy.start()
        sent.append(copy)

    def wait_for(slot, send_sem, recv_sem):
        remote(slot, slot, send_sem, recv_sem, sibling).wait_recv()

    def to_window(ref, send_sem, recv_sem):
        for wi, off in window_pairs:
            send(
                ref.at[0, y],
                ref.at[wi, y],
                send_sem.at[wi, off],
                recv_sem.at[wi, off],
                device(y_at(off), z_at(-WINDOW[wi]), x, c),
            )

    def from_window(ref, send_sem, recv_sem):
        for wi, off in window_pairs:
            wait_for(ref.at[wi, y_at(-off)], send_sem.at[wi, off], recv_sem.at[wi, off])

    def piece(wi, off):
        k = x_at(off)
        kind = lax.rem(z_at(-WINDOW[wi]), NW)
        first = k * PIECE
        row = 64 * (kind + NW * lax.div(first, 64)) + lax.rem(first, 64)
        return xt.at[pl.ds(pl.multiple_of(row, PIECE), PIECE)]

    def scatter(wi, off):
        k = x_at(off)
        return remote(
            piece(wi, off),
            xs.at[wi, y, k * 2 + c],
            sc_send.at[wi, off],
            sc_recv.at[wi, y],
            device(x, z_at(-WINDOW[wi]), k, c),
        )

    def grads_along_y(wi):
        block = gy.at[wi, y]
        send(block, block, gy_send.at[wi, 0], gy_recv.at[wi, 0], y_peer(1))
        send(block, block, gy_send.at[wi, 1], gy_recv.at[wi, 1], y_peer(-1))

    def grads_onward(wi):
        for way, step in ((0, 1), (1, -1)):
            block = gy.at[wi, y_at(-step)]
            wait_for(block, gy_send.at[wi, way], gy_recv.at[wi, way])
            half = gy.at[wi, y_at(-step), pl.ds(128 * way, 128)]
            send(half, half, gf_send.at[wi, way], gf_recv.at[wi, way], y_peer(step))

    to_window(hist, hist_send, hist_recv)

    own_piece = pltpu.make_async_copy(piece(0, 0), xs.at[0, y, tensor], sc_recv.at[0, y])
    own_scatter = scatter(0, 0)

    @pl.when(jnp.logical_not(on_diagonal))
    def _():
        own_scatter.start()

    @pl.when(on_diagonal)
    def _():
        own_piece.start()

    for wi, off in piece_pairs:
        copy = scatter(wi, off)
        copy.start()
        sent.append(copy)


    for off in range(1, NT):
        send(gp.at[t_at(off)], gr.at[tensor], gr_send.at[off], gr_recv.at[off], (dp, t_at(off)))

    for wi in range(1, NW):
        send(
            own_grads,
            gy.at[wi, y],
            gz_send.at[wi],
            gz_recv.at[wi],
            device(y, z_at(-WINDOW[wi]), x, c),
        )


    grads_along_y(0)

    span = NW * NY // BLOCKS
    blocks = [(b * span // NY, b * span % NY) for b in range(BLOCKS)]

    def block_of(b, source_x, source_c):
        wi, first = blocks[b]
        return xs.at[wi, pl.ds(first, span), source_x * 2 + source_c]

    for b in range(BLOCKS):
        wi, first = blocks[b]
        for yy in range(first, first + span):
            wait_for(xs.at[wi, yy, tensor], sc_send.at[0, 0], sc_recv.at[wi, yy])
        block = block_of(b, x, c)
        send(block, block, ag_send.at[0, b], ag_recv.at[0, b], x_peer(1))
        send(block, block, ag_send.at[1, b], ag_recv.at[1, b], x_peer(-1))
        send(block, block, sib_send.at[0, b], sib_recv.at[0, b], sibling)

    for wi in range(1, NW):
        wait_for(gy.at[wi, y], gz_send.at[wi], gz_recv.at[wi])
        grads_along_y(wi)

    from_window(hist, hist_send, hist_recv)
    window_count = hist[0, 0]
    for wi in range(NW):
        for yy in range(NY):
            if (wi, yy) != (0, 0):
                window_count = window_count + hist[wi, yy]
    ring[0] = window_count

    def ring_send_to(slot, src, target):
        send(ring.at[src], ring.at[slot], ring_send.at[slot], ring_recv.at[slot], target)

    def ring_wait(slot):
        wait_for(ring.at[slot], ring_send.at[slot], ring_recv.at[slot])

    for slot, target in ((3, below2), (4, above2), (1, below), (2, above)):
        ring_send_to(slot, 0, target)
    grads_onward(0)

    total = gp[tensor].astype(F32)
    for off in range(1, NT):
        source = t_at(-off)
        wait_for(gr.at[source], gr_send.at[off], gr_recv.at[off])
        total = total + gr[source].astype(F32)
    product = total[0] * total[1] + total[2] * total[3] + total[4] * total[5]
    band = (16, 128)
    packed_row = lax.broadcasted_iota(jnp.int32, band, 0) + tensor * 16
    packed_lane = lax.broadcasted_iota(jnp.int32, band, 1)
    inner_row = lax.rem(packed_row, 64)
    inner_lane = lax.rem(packed_lane, 64)
    base = 64 * (2 * lax.div(packed_row, 64) + lax.div(packed_lane, 64))
    tok_t = base + inner_row
    tok_s = base + inner_lane + jnp.where(inner_lane >= inner_row, 0, 64)
    product = product * jnp.where(tok_t == tok_s, 1.0, 2.0)
    norm_part = jnp.zeros(tile, F32)
    for d in range(MAXDOC):
        inside = (
            (tok_t >= starts[d]) & (tok_t < ends[d]) & (tok_s >= starts[d]) & (tok_s < ends[d])
        )
        value = jnp.sum(jnp.where(inside, product, 0.0), keepdims=True)
        norm_part = jnp.where(sub8 == d, value, norm_part)
    npr[tensor] = norm_part
    for off in range(1, NT):
        send(
            npr.at[tensor], npr.at[tensor], np_send.at[off], np_recv.at[off], (dp, t_at(off))
        )

    for slot in range(1, 5):
        ring_wait(slot)
    ring[5] = ring[1] + ring[3]
    ring_send_to(6, 5, below2)
    ring_send_to(7, 2, above2)

    for b in range(BLOCKS):
        for hop, step in ((0, 1), (1, -1)):
            block = block_of(b, x_at(-step), c)
            wait_for(block, ag_send.at[hop, b], ag_recv.at[hop, b])
            if (b < BLOCKS // 2) == (hop == 0):
                send(block, block, ag_send.at[2, b], ag_recv.at[2, b], x_peer(step))
            send(block, block, sib_send.at[hop + 1, b], sib_recv.at[hop + 1, b], sibling)

    for wi in range(1, NW):
        grads_onward(wi)

    ring_wait(6)
    ring_wait(7)
    counts = ring[0] + ring[6] + ring[7]
    for slot in range(1, 5):
        counts = counts + ring[slot]
    doc_count = jnp.sum(jnp.where(lane8 == patient_of, counts, 0.0), axis=1, keepdims=True)
    for off in range(1, NT):
        wait_for(npr.at[t_at(-off)], np_send.at[off], np_recv.at[off])
    norms = npr[0]
    for tt in range(1, NT):
        norms = norms + npr[tt]
    scale = clip_bound / jnp.maximum(clip_bound, jnp.sqrt(norms)) / jnp.maximum(doc_count, 1.0)
    position = lane8 + 128 * sub8
    weights = jnp.zeros(tile, F32)
    for d in range(MAXDOC):
        weights = jnp.where(
            (position >= starts[d]) & (position < ends[d]), scale[d : d + 1, :], weights
        )
    told[0, y] = weights
    to_window(told, told_send, told_recv)
    scale_row = jnp.sum(jnp.where(sub8 == lane8, scale, 0.0), axis=0, keepdims=True)
    scale_ref[...] = scale_row[:, :MAXDOC]

    for b in range(BLOCKS):
        block = block_of(b, x_at(2), c)
        wait_for(block, ag_send.at[2, b], ag_recv.at[2, b])
        send(block, block, sib_send.at[3, b], sib_recv.at[3, b], sibling)

    from_window(told, told_send, told_recv)
    columns = told[...].reshape(NW * NY * 8, 128).T
    for wi in range(NW):
        for way in range(2):
            half = gy.at[wi, y_at(2), pl.ds(128 * way, 128)]
            wait_for(half, gf_send.at[wi, way], gf_recv.at[wi, way])
        for yy in range(NY):
            for way in range(2):
                lane = (wi * NY + yy) * 8 + way
                rows = pl.ds(128 * way, 128)
                weight = columns[:, lane : lane + 1]
                wy[wi, yy, rows] = (weight * gy[wi, yy, rows].astype(F32)).astype(BF16)

    for hop, source_x in enumerate((x, x_at(-1), x_at(1), x_at(2))):
        for b in range(BLOCKS):
            wait_for(block_of(b, source_x, 1 - c), sib_send.at[hop, b], sib_recv.at[hop, b])

    sums = None
    for wi in range(NW):
        for yy in range(NY):
            features = xs[wi, yy].reshape(NT * PIECE, TOK)
            term = jnp.dot(features, wy[wi, yy], preferred_element_type=F32)
            sums = term if sums is None else sums + term
    step_rows = min(PIECE, 64)
    for tt in range(NT):
        for q in range(0, PIECE, step_rows):
            inner = (tt // 2) * PIECE + q
            owner = (tt % 2) * (8 // NW) + inner // 64
            first = tt * PIECE + q
            part[owner, inner % 64 : inner % 64 + step_rows] = sums[first : first + step_rows]

    rows = 64 // PIECES

    def owner_at(off):
        return lax.rem(place + off + members, members)

    def part_rows(off, j):
        return part.at[owner_at(off), pl.ds(j * rows, rows)]

    def arrival(slot, j):
        return sums_in.at[slot, pl.ds(j * rows, rows)]

    def sum_send(slot, j, off, target):
        send(
            part_rows(off, j),
            arrival(slot, j),
            sum_sent.at[slot, j],
            sum_recv.at[slot, j],
            target,
        )

    def sum_wait(slot, j):
        wait_for(arrival(slot, j), sum_sent.at[slot, j], sum_recv.at[slot, j])
        return arrival(slot, j)[...]

    for j in range(PIECES):
        if j % 2 == 0:
            sum_send(2, j, 4, below2)
        else:
            sum_send(3, j, 4, above2)
    for j in range(PIECES):
        sum_send(0, j, -3, below)
        sum_send(1, j, 3, above)
    for j in range(PIECES):
        sum_send(6, j, -1, below)
        sum_send(7, j, 1, above)

    for far in (False, True):
        for j in range(PIECES):
            for way in range(2):
                if far != (j % 2 == way):
                    continue
                near = (-2, 2)[way]
                value = sum_wait(way, j)
                if far:
                    value = value + sum_wait(2 + way, j)
                part_rows(near, j)[...] += value
                sum_send(4 + way, j, near, (below2, above2)[way])
    for j in range(PIECES):
        value = part[place, pl.ds(j * rows, rows), :]
        for slot in (6, 7, 4, 5):
            value = value + sum_wait(slot, j)
        out_ref[pl.ds(j * rows, rows), :] = value

    @pl.when(jnp.logical_not(on_diagonal))
    def _():
        own_scatter.wait_send()

    for copy in sent:
        copy.wait_send()


def on_device(nz, layer_inputs, layer_outgrads, doc_starts, row_tokens, doc_patient):
    clip_bound = DOC_MOST * math.sqrt(LAYERS * D * GW) / 300.0
    members = nz // NW
    assert members == 8
    vmem = pl.BlockSpec(memory_space=pltpu.VMEM)
    anywhere = pl.BlockSpec(memory_space=pl.ANY)
    dma = pltpu.SemaphoreType.DMA
    return pl.pallas_call(
        functools.partial(kernel, nz, clip_bound),
        out_shape=(
            jax.ShapeDtypeStruct((64, 256), F32),
            jax.ShapeDtypeStruct((1, MAXDOC), F32),
        ),
        in_specs=[anywhere] * 5,
        out_specs=(vmem, vmem),
        scratch_shapes=[
            pltpu.SMEM((1, MAXDOC), jnp.int32),
            pltpu.SMEM((1,), jnp.int32),
            pltpu.SMEM((1, MAXDOC), jnp.int32),
            pltpu.VMEM((LAYERS, TOK, 512), BF16),
            pltpu.VMEM((LAYERS - 1, TOK, 256), BF16),
            pltpu.VMEM((512, TOK), BF16),
            pltpu.VMEM((NW, NY, NT, PIECE, TOK), BF16),
            pltpu.VMEM((NW, NY, TOK, 256), BF16),
            pltpu.VMEM((NW, NY, TOK, 256), BF16),
            pltpu.VMEM((NT, 6, 16, 128), GRAM_TYPE),
            pltpu.VMEM((NT, 6, 16, 128), GRAM_TYPE),
            pltpu.VMEM((NT, 8, 128), F32),
            pltpu.VMEM((NW, NY, 8, 128), F32),
            pltpu.VMEM((8, 8, 128), F32),
            pltpu.VMEM((NW, NY, 8, 128), F32),
            pltpu.VMEM((members, 64, 256), F32),
            pltpu.VMEM((8, 64, 256), F32),
            dma((7,)),
            dma((NW, NX)),
            dma((NW, NY)),
            dma((NW,)),
            dma((NW,)),
            dma((NW, 2)),
            dma((NW, 2)),
            dma((NW, 2)),
            dma((NW, 2)),
            dma((NW, NY)),
            dma((NW, NY)),
            dma((8,)),
            dma((8,)),
            dma((NT,)),
            dma((NT,)),
            dma((NT,)),
            dma((NT,)),
            dma((NW, NY)),
            dma((NW, NY)),
            dma((3, BLOCKS)),
            dma((3, BLOCKS)),
            dma((4, BLOCKS)),
            dma((4, BLOCKS)),
            dma((8, PIECES)),
            dma((8, PIECES)),
        ],
        compiler_params=pltpu.CompilerParams(
            collective_id=0, has_side_effects=True, vmem_limit_bytes=VMEM_BYTES
        ),
    )(layer_inputs, layer_outgrads, doc_starts, row_tokens, doc_patient)


def solution(mesh):
    placed = (
        P(None, "dp", "tensor"),
        P(None, "dp", "tensor"),
        P("dp", None),
        P("dp"),
        P("dp", None),
    )
    return jax.shard_map(
        functools.partial(on_device, mesh.shape["dp"] // NY),
        mesh=mesh,
        in_specs=placed,
        out_specs=(P("dp", "tensor"), P("dp", None)),
        check_vma=False,
    )
```

```python
import functools
import math

import jax
import jax.numpy as jnp
from jax import lax
from jax.experimental import pallas as pl
from jax.experimental.pallas import tpu as pltpu
from jax.sharding import PartitionSpec as P

D = 4096
LAYERS = 3
DOC_MOST = 64
GW = 2048
MAXDOC = 8
TOK = 256
NX = 4
NY = 4
NT = 2 * NX
WINDOW = (0, 1)
NW = len(WINDOW)
PIECE = 128 // NW
BLOCKS = 4
PIECES = 2
VMEM_BYTES = 63283200
GRAM_TYPE = jnp.bfloat16
MESH = pl.DeviceIdType.MESH
F32 = jnp.float32
BF16 = jnp.bfloat16


def remote(src, dst, send_sem, recv_sem, device):
    return pltpu.make_async_remote_copy(
        src_ref=src,
        dst_ref=dst,
        send_sem=send_sem,
        recv_sem=recv_sem,
        device_id=device,
        device_id_type=MESH,
    )


def pack_band(gram):
    shape = (64, 128)
    row = lax.broadcasted_iota(jnp.int32, shape, 0)
    lane = lax.broadcasted_iota(jnp.int32, shape, 1)
    upper = lax.rem(lane, 64) >= row
    low_lanes = lane < 64
    halves = []
    for q in range(2):
        base = 128 * q
        first = gram[base : base + 64, base : base + 128]
        second = gram[base + 64 : base + 128, base : base + 128]
        block0 = jnp.where(upper, first, pltpu.roll(first, 64, 1))
        if q == 0:
            across = pltpu.roll(gram[base + 64 : base + 128, base + 128 : base + 256], 64, 1)
        else:
            across = jnp.zeros(shape, F32)
        block1 = jnp.where(upper, second, across)
        halves.append(jnp.where(low_lanes, block0, block1))
    return halves


def gram_of(block):
    return lax.dot_general(block, block, (((1,), (1,)), ((), ())), preferred_element_type=F32)


def kernel(
    nz,
    clip_bound,
    xi_ref,
    g_ref,
    starts_in,
    rows_in,
    pat_in,
    out_ref,
    scale_ref,
    starts_ref,
    rows_ref,
    pat_ref,
    xv,
    gv,
    xt,
    xs,
    gy,
    wy,
    gp,
    gr,
    npr,
    hist,
    ring,
    told,
    part,
    sums_in,
    in_sem,
    sc_send,
    sc_recv,
    gz_send,
    gz_recv,
    gy_send,
    gy_recv,
    gf_send,
    gf_recv,
    hist_send,
    hist_recv,
    ring_send,
    ring_recv,
    gr_send,
    gr_recv,
    np_send,
    np_recv,
    told_send,
    told_recv,
    ag_send,
    ag_recv,
    sib_send,
    sib_recv,
    sum_sent,
    sum_recv,
):
    dp = lax.axis_index("dp")
    tensor = lax.axis_index("tensor")
    y = lax.div(dp, nz)
    z = lax.rem(dp, nz)
    x = lax.div(tensor, 2)
    c = lax.rem(tensor, 2)
    members = 8
    place = lax.div(z, NW)

    def device(yy, zz, xx, cc):
        return (yy * nz + zz, xx * 2 + cc)

    def z_at(off):
        return lax.rem(z + off + nz, nz)

    def y_at(off):
        return lax.rem(y + off + NY, NY)

    def x_at(off):
        return lax.rem(x + off + NX, NX)

    def t_at(off):
        return lax.rem(tensor + off + NT, NT)

    def x_peer(off):
        return device(y, z, x_at(off), c)

    def y_peer(off):
        return device(y_at(off), z, x, c)

    sibling = device(y, z, x, 1 - c)
    below, above = device(y, z_at(-NW), x, c), device(y, z_at(NW), x, c)
    below2, above2 = device(y, z_at(-2 * NW), x, c), device(y, z_at(2 * NW), x, c)
    on_diagonal = x == y
    window_pairs = [(wi, off) for wi in range(NW) for off in range(NY) if (wi, off) != (0, 0)]
    piece_pairs = [(wi, off) for wi in range(NW) for off in range(NX) if (wi, off) != (0, 0)]

    barrier = pltpu.get_barrier_semaphore()

    def greet(target):
        pl.semaphore_signal(barrier, inc=1, device_id=target, device_id_type=MESH)

    for off in range(1, NT):
        greet((dp, t_at(off)))
    window_peers = {(off, way * d) for d in WINDOW for way in (1, -1) for off in range(NY)}
    window_peers = sorted(window_peers - {(0, 0)})
    for off, d in window_peers:
        greet(device(y_at(off), z_at(d), x, c))
    for wi, off in piece_pairs:
        greet(device(x, z_at(-WINDOW[wi]), x_at(off), c))
        greet(device(y_at(off), z_at(WINDOW[wi]), y, c))
    for target in (below, above, below2, above2):
        greet(target)

    @pl.when(jnp.logical_not(on_diagonal))
    def _():
        greet(device(x, z, x, c))
        greet(device(y, z, y, c))

    greetings = NT - 1 + len(window_peers) + 2 * len(piece_pairs) + 4

    own_grads = gy.at[0, y]
    loads = [
        pltpu.make_async_copy(xi_ref.at[0], xv.at[0], in_sem.at[0]),
        pltpu.make_async_copy(g_ref.at[0], own_grads, in_sem.at[1]),
        pltpu.make_async_copy(starts_in, starts_ref, in_sem.at[2]),
        pltpu.make_async_copy(rows_in, rows_ref, in_sem.at[3]),
        pltpu.make_async_copy(pat_in, pat_ref, in_sem.at[4]),
        pltpu.make_async_copy(xi_ref.at[pl.ds(1, 2)], xv.at[pl.ds(1, 2)], in_sem.at[5]),
        pltpu.make_async_copy(g_ref.at[pl.ds(1, 2)], gv, in_sem.at[6]),
    ]
    for copy in loads:
        copy.start()

    for copy in loads[2:5]:
        copy.wait()
    starts = [starts_ref[0, d] for d in range(MAXDOC)]
    used = rows_ref[0]
    ends = [jnp.minimum(starts[d + 1], used) if d + 1 < MAXDOC else used for d in range(MAXDOC)]
    patients = [pat_ref[0, d] for d in range(MAXDOC)]
    tile = (8, 128)
    sub8 = lax.broadcasted_iota(jnp.int32, tile, 0)
    lane8 = lax.broadcasted_iota(jnp.int32, tile, 1)
    own_hist = jnp.zeros(tile, F32)
    patient_of = jnp.zeros(tile, jnp.int32)
    for d in range(MAXDOC):
        nonempty = jnp.where(ends[d] > starts[d], 1.0, 0.0)
        own_hist = own_hist + jnp.where(lane8 == patients[d], nonempty, 0.0)
        patient_of = jnp.where(sub8 == d, patients[d], patient_of)
    hist[0, y] = own_hist

    def put_gram(which, block):
        low, high = pack_band(gram_of(block))
        for owner in range(NT):
            source = low if owner < 4 else high
            first = (owner % 4) * 16
            gp[owner, which] = source[first : first + 16].astype(GRAM_TYPE)

    loads[0].wait()
    xt[...] = xv[0].T
    put_gram(0, xv[0])
    loads[1].wait()
    put_gram(1, gy[0, y])
    loads[5].wait()
    loads[6].wait()
    for layer in range(1, LAYERS):
        put_gram(2 * layer, xv[layer])
        put_gram(2 * layer + 1, gv[layer - 1])

    pl.semaphore_wait(barrier, greetings + jnp.where(on_diagonal, 0, 2))

    sent = []

    def send(src, dst, send_sem, recv_sem, target):
        copy = remote(src, dst, send_sem, recv_sem, target)
        copy.start()
        sent.append(copy)

    def wait_for(slot, send_sem, recv_sem):
        remote(slot, slot, send_sem, recv_sem, sibling).wait_recv()

    def to_window(ref, send_sem, recv_sem):
        for wi, off in window_pairs:
            send(
                ref.at[0, y],
                ref.at[wi, y],
                send_sem.at[wi, off],
                recv_sem.at[wi, off],
                device(y_at(off), z_at(-WINDOW[wi]), x, c),
            )

    def from_window(ref, send_sem, recv_sem):
        for wi, off in window_pairs:
            wait_for(ref.at[wi, y_at(-off)], send_sem.at[wi, off], recv_sem.at[wi, off])

    def piece(wi, off):
        k = x_at(off)
        kind = lax.rem(z_at(-WINDOW[wi]), NW)
        first = k * PIECE
        row = 64 * (kind + NW * lax.div(first, 64)) + lax.rem(first, 64)
        return xt.at[pl.ds(pl.multiple_of(row, PIECE), PIECE)]

    def scatter(wi, off):
        k = x_at(off)
        return remote(
            piece(wi, off),
            xs.at[wi, y, k * 2 + c],
            sc_send.at[wi, off],
            sc_recv.at[wi, y],
            device(x, z_at(-WINDOW[wi]), k, c),
        )

    def grads_along_y(wi):
        block = gy.at[wi, y]
        send(block, block, gy_send.at[wi, 0], gy_recv.at[wi, 0], y_peer(1))
        send(block, block, gy_send.at[wi, 1], gy_recv.at[wi, 1], y_peer(-1))

    def grads_onward(wi):
        for way, step in ((0, 1), (1, -1)):
            block = gy.at[wi, y_at(-step)]
            wait_for(block, gy_send.at[wi, way], gy_recv.at[wi, way])
            half = gy.at[wi, y_at(-step), pl.ds(128 * way, 128)]
            send(half, half, gf_send.at[wi, way], gf_recv.at[wi, way], y_peer(step))

    to_window(hist, hist_send, hist_recv)

    own_piece = pltpu.make_async_copy(piece(0, 0), xs.at[0, y, tensor], sc_recv.at[0, y])
    own_scatter = scatter(0, 0)

    @pl.when(jnp.logical_not(on_diagonal))
    def _():
        own_scatter.start()

    @pl.when(on_diagonal)
    def _():
        own_piece.start()

    for wi, off in piece_pairs:
        copy = scatter(wi, off)
        copy.start()
        sent.append(copy)


    for off in range(1, NT):
        send(gp.at[t_at(off)], gr.at[tensor], gr_send.at[off], gr_recv.at[off], (dp, t_at(off)))

    for wi in range(1, NW):
        send(
            own_grads,
            gy.at[wi, y],
            gz_send.at[wi],
            gz_recv.at[wi],
            device(y, z_at(-WINDOW[wi]), x, c),
        )


    grads_along_y(0)

    from_window(hist, hist_send, hist_recv)
    window_count = hist[0, 0]
    for wi in range(NW):
        for yy in range(NY):
            if (wi, yy) != (0, 0):
                window_count = window_count + hist[wi, yy]
    ring[0] = window_count

    def ring_send_to(slot, src, target):
        send(ring.at[src], ring.at[slot], ring_send.at[slot], ring_recv.at[slot], target)

    def ring_wait(slot):
        wait_for(ring.at[slot], ring_send.at[slot], ring_recv.at[slot])

    for slot, target in ((3, below2), (4, above2), (1, below), (2, above)):
        ring_send_to(slot, 0, target)

    span = NW * NY // BLOCKS
    blocks = [(b * span // NY, b * span % NY) for b in range(BLOCKS)]

    def block_of(b, source_x, source_c):
        wi, first = blocks[b]
        return xs.at[wi, pl.ds(first, span), source_x * 2 + source_c]

    for b in range(BLOCKS):
        wi, first = blocks[b]
        for yy in range(first, first + span):
            wait_for(xs.at[wi, yy, tensor], sc_send.at[0, 0], sc_recv.at[wi, yy])
        block = block_of(b, x, c)
        send(block, block, ag_send.at[0, b], ag_recv.at[0, b], x_peer(1))
        send(block, block, ag_send.at[1, b], ag_recv.at[1, b], x_peer(-1))
        send(block, block, sib_send.at[0, b], sib_recv.at[0, b], sibling)

    for wi in range(1, NW):
        wait_for(gy.at[wi, y], gz_send.at[wi], gz_recv.at[wi])
        grads_along_y(wi)

    grads_onward(0)

    total = gp[tensor].astype(F32)
    for off in range(1, NT):
        source = t_at(-off)
        wait_for(gr.at[source], gr_send.at[off], gr_recv.at[off])
        total = total + gr[source].astype(F32)
    product = total[0] * total[1] + total[2] * total[3] + total[4] * total[5]
    band = (16, 128)
    packed_row = lax.broadcasted_iota(jnp.int32, band, 0) + tensor * 16
    packed_lane = lax.broadcasted_iota(jnp.int32, band, 1)
    inner_row = lax.rem(packed_row, 64)
    inner_lane = lax.rem(packed_lane, 64)
    base = 64 * (2 * lax.div(packed_row, 64) + lax.div(packed_lane, 64))
    tok_t = base + inner_row
    tok_s = base + inner_lane + jnp.where(inner_lane >= inner_row, 0, 64)
    product = product * jnp.where(tok_t == tok_s, 1.0, 2.0)
    norm_part = jnp.zeros(tile, F32)
    for d in range(MAXDOC):
        inside = (
            (tok_t >= starts[d]) & (tok_t < ends[d]) & (tok_s >= starts[d]) & (tok_s < ends[d])
        )
        value = jnp.sum(jnp.where(inside, product, 0.0), keepdims=True)
        norm_part = jnp.where(sub8 == d, value, norm_part)
    npr[tensor] = norm_part
    for off in range(1, NT):
        send(
            npr.at[tensor], npr.at[tensor], np_send.at[off], np_recv.at[off], (dp, t_at(off))
        )

    for slot in range(1, 5):
        ring_wait(slot)
    ring[5] = ring[1] + ring[3]
    ring_send_to(6, 5, below2)
    ring_send_to(7, 2, above2)

    for b in range(BLOCKS):
        for hop, step in ((0, 1), (1, -1)):
            block = block_of(b, x_at(-step), c)
            wait_for(block, ag_send.at[hop, b], ag_recv.at[hop, b])
            if (b < BLOCKS // 2) == (hop == 0):
                send(block, block, ag_send.at[2, b], ag_recv.at[2, b], x_peer(step))
            send(block, block, sib_send.at[hop + 1, b], sib_recv.at[hop + 1, b], sibling)

    for wi in range(1, NW):
        grads_onward(wi)

    ring_wait(6)
    ring_wait(7)
    counts = ring[0] + ring[6] + ring[7]
    for slot in range(1, 5):
        counts = counts + ring[slot]
    doc_count = jnp.sum(jnp.where(lane8 == patient_of, counts, 0.0), axis=1, keepdims=True)
    for off in range(1, NT):
        wait_for(npr.at[t_at(-off)], np_send.at[off], np_recv.at[off])
    norms = npr[0]
    for tt in range(1, NT):
        norms = norms + npr[tt]
    scale = clip_bound / jnp.maximum(clip_bound, jnp.sqrt(norms)) / jnp.maximum(doc_count, 1.0)
    position = lane8 + 128 * sub8
    weights = jnp.zeros(tile, F32)
    for d in range(MAXDOC):
        weights = jnp.where(
            (position >= starts[d]) & (position < ends[d]), scale[d : d + 1, :], weights
        )
    told[0, y] = weights
    to_window(told, told_send, told_recv)
    scale_row = jnp.sum(jnp.where(sub8 == lane8, scale, 0.0), axis=0, keepdims=True)
    scale_ref[...] = scale_row[:, :MAXDOC]

    for b in range(BLOCKS):
        block = block_of(b, x_at(2), c)
        wait_for(block, ag_send.at[2, b], ag_recv.at[2, b])
        send(block, block, sib_send.at[3, b], sib_recv.at[3, b], sibling)

    from_window(told, told_send, told_recv)
    columns = told[...].reshape(NW * NY * 8, 128).T
    for wi in range(NW):
        for way in range(2):
            half = gy.at[wi, y_at(2), pl.ds(128 * way, 128)]
            wait_for(half, gf_send.at[wi, way], gf_recv.at[wi, way])
        for yy in range(NY):
            for way in range(2):
                lane = (wi * NY + yy) * 8 + way
                rows = pl.ds(128 * way, 128)
                weight = columns[:, lane : lane + 1]
                wy[wi, yy, rows] = (weight * gy[wi, yy, rows].astype(F32)).astype(BF16)

    for hop, source_x in enumerate((x, x_at(-1), x_at(1), x_at(2))):
        for b in range(BLOCKS):
            wait_for(block_of(b, source_x, 1 - c), sib_send.at[hop, b], sib_recv.at[hop, b])

    sums = None
    for wi in range(NW):
        for yy in range(NY):
            features = xs[wi, yy].reshape(NT * PIECE, TOK)
            term = jnp.dot(features, wy[wi, yy], preferred_element_type=F32)
            sums = term if sums is None else sums + term
    step_rows = min(PIECE, 64)
    for tt in range(NT):
        for q in range(0, PIECE, step_rows):
            inner = (tt // 2) * PIECE + q
            owner = (tt % 2) * (8 // NW) + inner // 64
            first = tt * PIECE + q
            part[owner, inner % 64 : inner % 64 + step_rows] = sums[first : first + step_rows]

    rows = 64 // PIECES

    def owner_at(off):
        return lax.rem(place + off + members, members)

    def part_rows(off, j):
        return part.at[owner_at(off), pl.ds(j * rows, rows)]

    def arrival(slot, j):
        return sums_in.at[slot, pl.ds(j * rows, rows)]

    def sum_send(slot, j, off, target):
        send(
            part_rows(off, j),
            arrival(slot, j),
            sum_sent.at[slot, j],
            sum_recv.at[slot, j],
            target,
        )

    def sum_wait(slot, j):
        wait_for(arrival(slot, j), sum_sent.at[slot, j], sum_recv.at[slot, j])
        return arrival(slot, j)[...]

    for j in range(PIECES):
        if j % 2 == 0:
            sum_send(2, j, 4, below2)
        else:
            sum_send(3, j, 4, above2)
    for j in range(PIECES):
        sum_send(0, j, -3, below)
        sum_send(1, j, 3, above)
    for j in range(PIECES):
        sum_send(6, j, -1, below)
        sum_send(7, j, 1, above)

    for far in (False, True):
        for j in range(PIECES):
            for way in range(2):
                if far != (j % 2 == way):
                    continue
                near = (-2, 2)[way]
                value = sum_wait(way, j)
                if far:
                    value = value + sum_wait(2 + way, j)
                part_rows(near, j)[...] += value
                sum_send(4 + way, j, near, (below2, above2)[way])
    for j in range(PIECES):
        value = part[place, pl.ds(j * rows, rows), :]
        for slot in (6, 7, 4, 5):
            value = value + sum_wait(slot, j)
        out_ref[pl.ds(j * rows, rows), :] = value

    @pl.when(jnp.logical_not(on_diagonal))
    def _():
        own_scatter.wait_send()

    for copy in sent:
        copy.wait_send()


def on_device(nz, layer_inputs, layer_outgrads, doc_starts, row_tokens, doc_patient):
    clip_bound = DOC_MOST * math.sqrt(LAYERS * D * GW) / 300.0
    members = nz // NW
    assert members == 8
    vmem = pl.BlockSpec(memory_space=pltpu.VMEM)
    anywhere = pl.BlockSpec(memory_space=pl.ANY)
    dma = pltpu.SemaphoreType.DMA
    return pl.pallas_call(
        functools.partial(kernel, nz, clip_bound),
        out_shape=(
            jax.ShapeDtypeStruct((64, 256), F32),
            jax.ShapeDtypeStruct((1, MAXDOC), F32),
        ),
        in_specs=[anywhere] * 5,
        out_specs=(vmem, vmem),
        scratch_shapes=[
            pltpu.SMEM((1, MAXDOC), jnp.int32),
            pltpu.SMEM((1,), jnp.int32),
            pltpu.SMEM((1, MAXDOC), jnp.int32),
            pltpu.VMEM((LAYERS, TOK, 512), BF16),
            pltpu.VMEM((LAYERS - 1, TOK, 256), BF16),
            pltpu.VMEM((512, TOK), BF16),
            pltpu.VMEM((NW, NY, NT, PIECE, TOK), BF16),
            pltpu.VMEM((NW, NY, TOK, 256), BF16),
            pltpu.VMEM((NW, NY, TOK, 256), BF16),
            pltpu.VMEM((NT, 6, 16, 128), GRAM_TYPE),
            pltpu.VMEM((NT, 6, 16, 128), GRAM_TYPE),
            pltpu.VMEM((NT, 8, 128), F32),
            pltpu.VMEM((NW, NY, 8, 128), F32),
            pltpu.VMEM((8, 8, 128), F32),
            pltpu.VMEM((NW, NY, 8, 128), F32),
            pltpu.VMEM((members, 64, 256), F32),
            pltpu.VMEM((8, 64, 256), F32),
            dma((7,)),
            dma((NW, NX)),
            dma((NW, NY)),
            dma((NW,)),
            dma((NW,)),
            dma((NW, 2)),
            dma((NW, 2)),
            dma((NW, 2)),
            dma((NW, 2)),
            dma((NW, NY)),
            dma((NW, NY)),
            dma((8,)),
            dma((8,)),
            dma((NT,)),
            dma((NT,)),
            dma((NT,)),
            dma((NT,)),
            dma((NW, NY)),
            dma((NW, NY)),
            dma((3, BLOCKS)),
            dma((3, BLOCKS)),
            dma((4, BLOCKS)),
            dma((4, BLOCKS)),
            dma((8, PIECES)),
            dma((8, PIECES)),
        ],
        compiler_params=pltpu.CompilerParams(
            collective_id=0, has_side_effects=True, vmem_limit_bytes=VMEM_BYTES
        ),
    )(layer_inputs, layer_outgrads, doc_starts, row_tokens, doc_patient)


def solution(mesh):
    placed = (
        P(None, "dp", "tensor"),
        P(None, "dp", "tensor"),
        P("dp", None),
        P("dp"),
        P("dp", None),
    )
    return jax.shard_map(
        functools.partial(on_device, mesh.shape["dp"] // NY),
        mesh=mesh,
        in_specs=placed,
        out_specs=(P("dp", "tensor"), P("dp", None)),
        check_vma=False,
    )
```

```python
import functools
import math

import jax
import jax.numpy as jnp
from jax import lax
from jax.experimental import pallas as pl
from jax.experimental.pallas import tpu as pltpu
from jax.sharding import PartitionSpec as P

D = 4096
LAYERS = 3
DOC_MOST = 64
GW = 2048
MAXDOC = 8
TOK = 256
NX = 4
NY = 4
NT = 2 * NX
WINDOW = (0, 1)
NW = len(WINDOW)
PIECE = 128 // NW
BLOCKS = 4
PIECES = 2
VMEM_BYTES = 63283200
GRAM_TYPE = jnp.bfloat16
MESH = pl.DeviceIdType.MESH
F32 = jnp.float32
BF16 = jnp.bfloat16


def remote(src, dst, send_sem, recv_sem, device):
    return pltpu.make_async_remote_copy(
        src_ref=src,
        dst_ref=dst,
        send_sem=send_sem,
        recv_sem=recv_sem,
        device_id=device,
        device_id_type=MESH,
    )


def pack_band(gram):
    shape = (64, 128)
    row = lax.broadcasted_iota(jnp.int32, shape, 0)
    lane = lax.broadcasted_iota(jnp.int32, shape, 1)
    upper = lax.rem(lane, 64) >= row
    low_lanes = lane < 64
    halves = []
    for q in range(2):
        base = 128 * q
        first = gram[base : base + 64, base : base + 128]
        second = gram[base + 64 : base + 128, base : base + 128]
        block0 = jnp.where(upper, first, pltpu.roll(first, 64, 1))
        if q == 0:
            across = pltpu.roll(gram[base + 64 : base + 128, base + 128 : base + 256], 64, 1)
        else:
            across = jnp.zeros(shape, F32)
        block1 = jnp.where(upper, second, across)
        halves.append(jnp.where(low_lanes, block0, block1))
    return halves


def gram_of(block):
    return lax.dot_general(block, block, (((1,), (1,)), ((), ())), preferred_element_type=F32)


def kernel(
    nz,
    clip_bound,
    xi_ref,
    g_ref,
    starts_in,
    rows_in,
    pat_in,
    out_ref,
    scale_ref,
    starts_ref,
    rows_ref,
    pat_ref,
    xv,
    gv,
    xt,
    xs,
    gy,
    gp,
    gr,
    npr,
    hist,
    ring,
    told,
    part,
    sums_in,
    in_sem,
    sc_send,
    sc_recv,
    gz_send,
    gz_recv,
    gy_send,
    gy_recv,
    gf_send,
    gf_recv,
    hist_send,
    hist_recv,
    ring_send,
    ring_recv,
    gr_send,
    gr_recv,
    np_send,
    np_recv,
    told_send,
    told_recv,
    ag_send,
    ag_recv,
    sib_send,
    sib_recv,
    sum_sent,
    sum_recv,
):
    dp = lax.axis_index("dp")
    tensor = lax.axis_index("tensor")
    y = lax.div(dp, nz)
    z = lax.rem(dp, nz)
    x = lax.div(tensor, 2)
    c = lax.rem(tensor, 2)
    members = 8
    place = lax.div(z, NW)

    def device(yy, zz, xx, cc):
        return (yy * nz + zz, xx * 2 + cc)

    def z_at(off):
        return lax.rem(z + off + nz, nz)

    def y_at(off):
        return lax.rem(y + off + NY, NY)

    def x_at(off):
        return lax.rem(x + off + NX, NX)

    def t_at(off):
        return lax.rem(tensor + off + NT, NT)

    def x_peer(off):
        return device(y, z, x_at(off), c)

    def y_peer(off):
        return device(y_at(off), z, x, c)

    sibling = device(y, z, x, 1 - c)
    below, above = device(y, z_at(-NW), x, c), device(y, z_at(NW), x, c)
    below2, above2 = device(y, z_at(-2 * NW), x, c), device(y, z_at(2 * NW), x, c)
    on_diagonal = x == y
    window_pairs = [(wi, off) for wi in range(NW) for off in range(NY) if (wi, off) != (0, 0)]
    piece_pairs = [(wi, off) for wi in range(NW) for off in range(NX) if (wi, off) != (0, 0)]

    barrier = pltpu.get_barrier_semaphore()

    def greet(target):
        pl.semaphore_signal(barrier, inc=1, device_id=target, device_id_type=MESH)

    for off in range(1, NT):
        greet((dp, t_at(off)))
    window_peers = {(off, way * d) for d in WINDOW for way in (1, -1) for off in range(NY)}
    window_peers = sorted(window_peers - {(0, 0)})
    for off, d in window_peers:
        greet(device(y_at(off), z_at(d), x, c))
    for wi, off in piece_pairs:
        greet(device(x, z_at(-WINDOW[wi]), x_at(off), c))
        greet(device(y_at(off), z_at(WINDOW[wi]), y, c))
    for target in (below, above, below2, above2):
        greet(target)

    @pl.when(jnp.logical_not(on_diagonal))
    def _():
        greet(device(x, z, x, c))
        greet(device(y, z, y, c))

    greetings = NT - 1 + len(window_peers) + 2 * len(piece_pairs) + 4

    own_grads = gy.at[0, y]
    loads = [
        pltpu.make_async_copy(xi_ref.at[0], xv.at[0], in_sem.at[0]),
        pltpu.make_async_copy(g_ref.at[0], own_grads, in_sem.at[1]),
        pltpu.make_async_copy(starts_in, starts_ref, in_sem.at[2]),
        pltpu.make_async_copy(rows_in, rows_ref, in_sem.at[3]),
        pltpu.make_async_copy(pat_in, pat_ref, in_sem.at[4]),
        pltpu.make_async_copy(xi_ref.at[pl.ds(1, 2)], xv.at[pl.ds(1, 2)], in_sem.at[5]),
        pltpu.make_async_copy(g_ref.at[pl.ds(1, 2)], gv, in_sem.at[6]),
    ]
    for copy in loads:
        copy.start()

    for copy in loads[2:5]:
        copy.wait()
    starts = [starts_ref[0, d] for d in range(MAXDOC)]
    used = rows_ref[0]
    ends = [jnp.minimum(starts[d + 1], used) if d + 1 < MAXDOC else used for d in range(MAXDOC)]
    patients = [pat_ref[0, d] for d in range(MAXDOC)]
    tile = (8, 128)
    sub8 = lax.broadcasted_iota(jnp.int32, tile, 0)
    lane8 = lax.broadcasted_iota(jnp.int32, tile, 1)
    own_hist = jnp.zeros(tile, F32)
    patient_of = jnp.zeros(tile, jnp.int32)
    for d in range(MAXDOC):
        nonempty = jnp.where(ends[d] > starts[d], 1.0, 0.0)
        own_hist = own_hist + jnp.where(lane8 == patients[d], nonempty, 0.0)
        patient_of = jnp.where(sub8 == d, patients[d], patient_of)
    hist[0, y] = own_hist

    def put_gram(which, block):
        low, high = pack_band(gram_of(block))
        for owner in range(NT):
            source = low if owner < 4 else high
            first = (owner % 4) * 16
            gp[owner, which] = source[first : first + 16].astype(GRAM_TYPE)

    loads[0].wait()
    xt[...] = xv[0].T
    put_gram(0, xv[0])
    loads[1].wait()
    put_gram(1, gy[0, y])
    loads[5].wait()
    loads[6].wait()
    for layer in range(1, LAYERS):
        put_gram(2 * layer, xv[layer])
        put_gram(2 * layer + 1, gv[layer - 1])

    pl.semaphore_wait(barrier, greetings + jnp.where(on_diagonal, 0, 2))

    sent = []

    def send(src, dst, send_sem, recv_sem, target):
        copy = remote(src, dst, send_sem, recv_sem, target)
        copy.start()
        sent.append(copy)

    def wait_for(slot, send_sem, recv_sem):
        remote(slot, slot, send_sem, recv_sem, sibling).wait_recv()

    def to_window(ref, send_sem, recv_sem):
        for wi, off in window_pairs:
            send(
                ref.at[0, y],
                ref.at[wi, y],
                send_sem.at[wi, off],
                recv_sem.at[wi, off],
                device(y_at(off), z_at(-WINDOW[wi]), x, c),
            )

    def from_window(ref, send_sem, recv_sem):
        for wi, off in window_pairs:
            wait_for(ref.at[wi, y_at(-off)], send_sem.at[wi, off], recv_sem.at[wi, off])

    def piece(wi, off):
        k = x_at(off)
        kind = lax.rem(z_at(-WINDOW[wi]), NW)
        first = k * PIECE
        row = 64 * (kind + NW * lax.div(first, 64)) + lax.rem(first, 64)
        return xt.at[pl.ds(pl.multiple_of(row, PIECE), PIECE)]

    def scatter(wi, off):
        k = x_at(off)
        return remote(
            piece(wi, off),
            xs.at[wi, y, k * 2 + c],
            sc_send.at[wi, off],
            sc_recv.at[wi, y],
            device(x, z_at(-WINDOW[wi]), k, c),
        )

    def grads_along_y(wi):
        block = gy.at[wi, y]
        send(block, block, gy_send.at[wi, 0], gy_recv.at[wi, 0], y_peer(1))
        send(block, block, gy_send.at[wi, 1], gy_recv.at[wi, 1], y_peer(-1))

    def grads_onward(wi):
        for way, step in ((0, 1), (1, -1)):
            block = gy.at[wi, y_at(-step)]
            wait_for(block, gy_send.at[wi, way], gy_recv.at[wi, way])
            half = gy.at[wi, y_at(-step), pl.ds(128 * way, 128)]
            send(half, half, gf_send.at[wi, way], gf_recv.at[wi, way], y_peer(step))

    to_window(hist, hist_send, hist_recv)

    own_piece = pltpu.make_async_copy(piece(0, 0), xs.at[0, y, tensor], sc_recv.at[0, y])
    own_scatter = scatter(0, 0)

    @pl.when(jnp.logical_not(on_diagonal))
    def _():
        own_scatter.start()

    @pl.when(on_diagonal)
    def _():
        own_piece.start()

    for wi, off in piece_pairs:
        copy = scatter(wi, off)
        copy.start()
        sent.append(copy)


    for off in range(1, NT):
        send(gp.at[t_at(off)], gr.at[tensor], gr_send.at[off], gr_recv.at[off], (dp, t_at(off)))

    for wi in range(1, NW):
        send(
            own_grads,
            gy.at[wi, y],
            gz_send.at[wi],
            gz_recv.at[wi],
            device(y, z_at(-WINDOW[wi]), x, c),
        )


    grads_along_y(0)

    from_window(hist, hist_send, hist_recv)
    window_count = hist[0, 0]
    for wi in range(NW):
        for yy in range(NY):
            if (wi, yy) != (0, 0):
                window_count = window_count + hist[wi, yy]
    ring[0] = window_count

    def ring_send_to(slot, src, target):
        send(ring.at[src], ring.at[slot], ring_send.at[slot], ring_recv.at[slot], target)

    def ring_wait(slot):
        wait_for(ring.at[slot], ring_send.at[slot], ring_recv.at[slot])

    for slot, target in ((3, below2), (4, above2), (1, below), (2, above)):
        ring_send_to(slot, 0, target)

    span = NW * NY // BLOCKS
    blocks = [(b * span // NY, b * span % NY) for b in range(BLOCKS)]

    def block_of(b, source_x, source_c):
        wi, first = blocks[b]
        return xs.at[wi, pl.ds(first, span), source_x * 2 + source_c]

    for b in range(BLOCKS):
        wi, first = blocks[b]
        for yy in range(first, first + span):
            wait_for(xs.at[wi, yy, tensor], sc_send.at[0, 0], sc_recv.at[wi, yy])
        block = block_of(b, x, c)
        send(block, block, ag_send.at[0, b], ag_recv.at[0, b], x_peer(1))
        send(block, block, ag_send.at[1, b], ag_recv.at[1, b], x_peer(-1))
        send(block, block, sib_send.at[0, b], sib_recv.at[0, b], sibling)

    for wi in range(1, NW):
        wait_for(gy.at[wi, y], gz_send.at[wi], gz_recv.at[wi])
        grads_along_y(wi)

    grads_onward(0)

    total = gp[tensor].astype(F32)
    for off in range(1, NT):
        source = t_at(-off)
        wait_for(gr.at[source], gr_send.at[off], gr_recv.at[off])
        total = total + gr[source].astype(F32)
    product = total[0] * total[1] + total[2] * total[3] + total[4] * total[5]
    band = (16, 128)
    packed_row = lax.broadcasted_iota(jnp.int32, band, 0) + tensor * 16
    packed_lane = lax.broadcasted_iota(jnp.int32, band, 1)
    inner_row = lax.rem(packed_row, 64)
    inner_lane = lax.rem(packed_lane, 64)
    base = 64 * (2 * lax.div(packed_row, 64) + lax.div(packed_lane, 64))
    tok_t = base + inner_row
    tok_s = base + inner_lane + jnp.where(inner_lane >= inner_row, 0, 64)
    product = product * jnp.where(tok_t == tok_s, 1.0, 2.0)
    norm_part = jnp.zeros(tile, F32)
    for d in range(MAXDOC):
        inside = (
            (tok_t >= starts[d]) & (tok_t < ends[d]) & (tok_s >= starts[d]) & (tok_s < ends[d])
        )
        value = jnp.sum(jnp.where(inside, product, 0.0), keepdims=True)
        norm_part = jnp.where(sub8 == d, value, norm_part)
    npr[tensor] = norm_part
    for off in range(1, NT):
        send(
            npr.at[tensor], npr.at[tensor], np_send.at[off], np_recv.at[off], (dp, t_at(off))
        )

    for slot in range(1, 5):
        ring_wait(slot)
    ring[5] = ring[1] + ring[3]
    ring_send_to(6, 5, below2)
    ring_send_to(7, 2, above2)

    for b in range(BLOCKS):
        for hop, step in ((0, 1), (1, -1)):
            block = block_of(b, x_at(-step), c)
            wait_for(block, ag_send.at[hop, b], ag_recv.at[hop, b])
            if (b < BLOCKS // 2) == (hop == 0):
                send(block, block, ag_send.at[2, b], ag_recv.at[2, b], x_peer(step))
            send(block, block, sib_send.at[hop + 1, b], sib_recv.at[hop + 1, b], sibling)

    for wi in range(1, NW):
        grads_onward(wi)

    ring_wait(6)
    ring_wait(7)
    counts = ring[0] + ring[6] + ring[7]
    for slot in range(1, 5):
        counts = counts + ring[slot]
    doc_count = jnp.sum(jnp.where(lane8 == patient_of, counts, 0.0), axis=1, keepdims=True)
    for off in range(1, NT):
        wait_for(npr.at[t_at(-off)], np_send.at[off], np_recv.at[off])
    norms = npr[0]
    for tt in range(1, NT):
        norms = norms + npr[tt]
    scale = clip_bound / jnp.maximum(clip_bound, jnp.sqrt(norms)) / jnp.maximum(doc_count, 1.0)
    position = lane8 + 128 * sub8
    weights = jnp.zeros(tile, F32)
    for d in range(MAXDOC):
        weights = jnp.where(
            (position >= starts[d]) & (position < ends[d]), scale[d : d + 1, :], weights
        )
    told[0, y] = weights
    to_window(told, told_send, told_recv)
    scale_row = jnp.sum(jnp.where(sub8 == lane8, scale, 0.0), axis=0, keepdims=True)
    scale_ref[...] = scale_row[:, :MAXDOC]

    for b in range(BLOCKS):
        block = block_of(b, x_at(2), c)
        wait_for(block, ag_send.at[2, b], ag_recv.at[2, b])
        send(block, block, sib_send.at[3, b], sib_recv.at[3, b], sibling)

    from_window(told, told_send, told_recv)
    columns = told[...].reshape(NW * NY * 8, 128).T
    for wi in range(NW):
        for way in range(2):
            half = gy.at[wi, y_at(2), pl.ds(128 * way, 128)]
            wait_for(half, gf_send.at[wi, way], gf_recv.at[wi, way])

    for hop, source_x in enumerate((x, x_at(-1), x_at(1), x_at(2))):
        for b in range(BLOCKS):
            wait_for(block_of(b, source_x, 1 - c), sib_send.at[hop, b], sib_recv.at[hop, b])

    sums = None
    for wi in range(NW):
        for yy in range(NY):
            features = xs[wi, yy].reshape(NT * PIECE, TOK)
            lane = (wi * NY + yy) * 8
            weight = jnp.concatenate([columns[:, lane : lane + 1], columns[:, lane + 1 : lane + 2]])
            weighted = (weight * gy[wi, yy].astype(F32)).astype(BF16)
            term = jnp.dot(features, weighted, preferred_element_type=F32)
            sums = term if sums is None else sums + term
    step_rows = min(PIECE, 64)
    for tt in range(NT):
        for q in range(0, PIECE, step_rows):
            inner = (tt // 2) * PIECE + q
            owner = (tt % 2) * (8 // NW) + inner // 64
            first = tt * PIECE + q
            part[owner, inner % 64 : inner % 64 + step_rows] = sums[first : first + step_rows]

    rows = 64 // PIECES

    def owner_at(off):
        return lax.rem(place + off + members, members)

    def part_rows(off, j):
        return part.at[owner_at(off), pl.ds(j * rows, rows)]

    def arrival(slot, j):
        return sums_in.at[slot, pl.ds(j * rows, rows)]

    def sum_send(slot, j, off, target):
        send(
            part_rows(off, j),
            arrival(slot, j),
            sum_sent.at[slot, j],
            sum_recv.at[slot, j],
            target,
        )

    def sum_wait(slot, j):
        wait_for(arrival(slot, j), sum_sent.at[slot, j], sum_recv.at[slot, j])
        return arrival(slot, j)[...]

    for j in range(PIECES):
        if j % 2 == 0:
            sum_send(2, j, 4, below2)
        else:
            sum_send(3, j, 4, above2)
    for j in range(PIECES):
        sum_send(0, j, -3, below)
        sum_send(1, j, 3, above)
    for j in range(PIECES):
        sum_send(6, j, -1, below)
        sum_send(7, j, 1, above)

    for far in (False, True):
        for j in range(PIECES):
            for way in range(2):
                if far != (j % 2 == way):
                    continue
                near = (-2, 2)[way]
                value = sum_wait(way, j)
                if far:
                    value = value + sum_wait(2 + way, j)
                part_rows(near, j)[...] += value
                sum_send(4 + way, j, near, (below2, above2)[way])
    for j in range(PIECES):
        value = part[place, pl.ds(j * rows, rows), :]
        for slot in (6, 7, 4, 5):
            value = value + sum_wait(slot, j)
        out_ref[pl.ds(j * rows, rows), :] = value

    @pl.when(jnp.logical_not(on_diagonal))
    def _():
        own_scatter.wait_send()

    for copy in sent:
        copy.wait_send()


def on_device(nz, layer_inputs, layer_outgrads, doc_starts, row_tokens, doc_patient):
    clip_bound = DOC_MOST * math.sqrt(LAYERS * D * GW) / 300.0
    members = nz // NW
    assert members == 8
    vmem = pl.BlockSpec(memory_space=pltpu.VMEM)
    anywhere = pl.BlockSpec(memory_space=pl.ANY)
    dma = pltpu.SemaphoreType.DMA
    return pl.pallas_call(
        functools.partial(kernel, nz, clip_bound),
        out_shape=(
            jax.ShapeDtypeStruct((64, 256), F32),
            jax.ShapeDtypeStruct((1, MAXDOC), F32),
        ),
        in_specs=[anywhere] * 5,
        out_specs=(vmem, vmem),
        scratch_shapes=[
            pltpu.SMEM((1, MAXDOC), jnp.int32),
            pltpu.SMEM((1,), jnp.int32),
            pltpu.SMEM((1, MAXDOC), jnp.int32),
            pltpu.VMEM((LAYERS, TOK, 512), BF16),
            pltpu.VMEM((LAYERS - 1, TOK, 256), BF16),
            pltpu.VMEM((512, TOK), BF16),
            pltpu.VMEM((NW, NY, NT, PIECE, TOK), BF16),
            pltpu.VMEM((NW, NY, TOK, 256), BF16),
            pltpu.VMEM((NT, 6, 16, 128), GRAM_TYPE),
            pltpu.VMEM((NT, 6, 16, 128), GRAM_TYPE),
            pltpu.VMEM((NT, 8, 128), F32),
            pltpu.VMEM((NW, NY, 8, 128), F32),
            pltpu.VMEM((8, 8, 128), F32),
            pltpu.VMEM((NW, NY, 8, 128), F32),
            pltpu.VMEM((members, 64, 256), F32),
            pltpu.VMEM((8, 64, 256), F32),
            dma((7,)),
            dma((NW, NX)),
            dma((NW, NY)),
            dma((NW,)),
            dma((NW,)),
            dma((NW, 2)),
            dma((NW, 2)),
            dma((NW, 2)),
            dma((NW, 2)),
            dma((NW, NY)),
            dma((NW, NY)),
            dma((8,)),
            dma((8,)),
            dma((NT,)),
            dma((NT,)),
            dma((NT,)),
            dma((NT,)),
            dma((NW, NY)),
            dma((NW, NY)),
            dma((3, BLOCKS)),
            dma((3, BLOCKS)),
            dma((4, BLOCKS)),
            dma((4, BLOCKS)),
            dma((8, PIECES)),
            dma((8, PIECES)),
        ],
        compiler_params=pltpu.CompilerParams(
            collective_id=0, has_side_effects=True, vmem_limit_bytes=VMEM_BYTES
        ),
    )(layer_inputs, layer_outgrads, doc_starts, row_tokens, doc_patient)


def solution(mesh):
    placed = (
        P(None, "dp", "tensor"),
        P(None, "dp", "tensor"),
        P("dp", None),
        P("dp"),
        P("dp", None),
    )
    return jax.shard_map(
        functools.partial(on_device, mesh.shape["dp"] // NY),
        mesh=mesh,
        in_specs=placed,
        out_specs=(P("dp", "tensor"), P("dp", None)),
        check_vma=False,
    )
```

```python
import functools
import math

import jax
import jax.numpy as jnp
from jax import lax
from jax.experimental import pallas as pl
from jax.experimental.pallas import tpu as pltpu
from jax.sharding import PartitionSpec as P

D = 4096
LAYERS = 3
DOC_MOST = 64
GW = 2048
MAXDOC = 8
TOK = 256
NX = 4
NY = 4
NT = 2 * NX
WINDOW = (0, 1)
NW = len(WINDOW)
PIECE = 128 // NW
BLOCKS = 4
PIECES = 4
VMEM_BYTES = 63283200
GRAM_TYPE = jnp.bfloat16
MESH = pl.DeviceIdType.MESH
F32 = jnp.float32
BF16 = jnp.bfloat16


def remote(src, dst, send_sem, recv_sem, device):
    return pltpu.make_async_remote_copy(
        src_ref=src,
        dst_ref=dst,
        send_sem=send_sem,
        recv_sem=recv_sem,
        device_id=device,
        device_id_type=MESH,
    )


def pack_band(gram):
    shape = (64, 128)
    row = lax.broadcasted_iota(jnp.int32, shape, 0)
    lane = lax.broadcasted_iota(jnp.int32, shape, 1)
    upper = lax.rem(lane, 64) >= row
    low_lanes = lane < 64
    halves = []
    for q in range(2):
        base = 128 * q
        first = gram[base : base + 64, base : base + 128]
        second = gram[base + 64 : base + 128, base : base + 128]
        block0 = jnp.where(upper, first, pltpu.roll(first, 64, 1))
        if q == 0:
            across = pltpu.roll(gram[base + 64 : base + 128, base + 128 : base + 256], 64, 1)
        else:
            across = jnp.zeros(shape, F32)
        block1 = jnp.where(upper, second, across)
        halves.append(jnp.where(low_lanes, block0, block1))
    return halves


def gram_of(block):
    return lax.dot_general(block, block, (((1,), (1,)), ((), ())), preferred_element_type=F32)


def kernel(
    nz,
    clip_bound,
    xi_ref,
    g_ref,
    starts_in,
    rows_in,
    pat_in,
    out_ref,
    scale_ref,
    starts_ref,
    rows_ref,
    pat_ref,
    xv,
    gv,
    xt,
    xs,
    gy,
    wy,
    gp,
    gr,
    npr,
    hist,
    ring,
    told,
    part,
    sums_in,
    in_sem,
    sc_send,
    sc_recv,
    gz_send,
    gz_recv,
    gy_send,
    gy_recv,
    gf_send,
    gf_recv,
    hist_send,
    hist_recv,
    ring_send,
    ring_recv,
    gr_send,
    gr_recv,
    np_send,
    np_recv,
    told_send,
    told_recv,
    ag_send,
    ag_recv,
    sib_send,
    sib_recv,
    sum_sent,
    sum_recv,
):
    dp = lax.axis_index("dp")
    tensor = lax.axis_index("tensor")
    y = lax.div(dp, nz)
    z = lax.rem(dp, nz)
    x = lax.div(tensor, 2)
    c = lax.rem(tensor, 2)
    members = 8
    place = lax.div(z, NW)

    def device(yy, zz, xx, cc):
        return (yy * nz + zz, xx * 2 + cc)

    def z_at(off):
        return lax.rem(z + off + nz, nz)

    def y_at(off):
        return lax.rem(y + off + NY, NY)

    def x_at(off):
        return lax.rem(x + off + NX, NX)

    def t_at(off):
        return lax.rem(tensor + off + NT, NT)

    def x_peer(off):
        return device(y, z, x_at(off), c)

    def y_peer(off):
        return device(y_at(off), z, x, c)

    sibling = device(y, z, x, 1 - c)
    below, above = device(y, z_at(-NW), x, c), device(y, z_at(NW), x, c)
    below2, above2 = device(y, z_at(-2 * NW), x, c), device(y, z_at(2 * NW), x, c)
    on_diagonal = x == y
    window_pairs = [(wi, off) for wi in range(NW) for off in range(NY) if (wi, off) != (0, 0)]
    piece_pairs = [(wi, off) for wi in range(NW) for off in range(NX) if (wi, off) != (0, 0)]

    barrier = pltpu.get_barrier_semaphore()

    def greet(target):
        pl.semaphore_signal(barrier, inc=1, device_id=target, device_id_type=MESH)

    for off in range(1, NT):
        greet((dp, t_at(off)))
    window_peers = {(off, way * d) for d in WINDOW for way in (1, -1) for off in range(NY)}
    window_peers = sorted(window_peers - {(0, 0)})
    for off, d in window_peers:
        greet(device(y_at(off), z_at(d), x, c))
    for wi, off in piece_pairs:
        greet(device(x, z_at(-WINDOW[wi]), x_at(off), c))
        greet(device(y_at(off), z_at(WINDOW[wi]), y, c))
    for target in (below, above, below2, above2):
        greet(target)

    @pl.when(jnp.logical_not(on_diagonal))
    def _():
        greet(device(x, z, x, c))
        greet(device(y, z, y, c))

    greetings = NT - 1 + len(window_peers) + 2 * len(piece_pairs) + 4

    own_grads = gy.at[0, y]
    loads = [
        pltpu.make_async_copy(xi_ref.at[0], xv.at[0], in_sem.at[0]),
        pltpu.make_async_copy(g_ref.at[0], own_grads, in_sem.at[1]),
        pltpu.make_async_copy(starts_in, starts_ref, in_sem.at[2]),
        pltpu.make_async_copy(rows_in, rows_ref, in_sem.at[3]),
        pltpu.make_async_copy(pat_in, pat_ref, in_sem.at[4]),
        pltpu.make_async_copy(xi_ref.at[pl.ds(1, 2)], xv.at[pl.ds(1, 2)], in_sem.at[5]),
        pltpu.make_async_copy(g_ref.at[pl.ds(1, 2)], gv, in_sem.at[6]),
    ]
    for copy in loads:
        copy.start()

    for copy in loads[2:5]:
        copy.wait()
    starts = [starts_ref[0, d] for d in range(MAXDOC)]
    used = rows_ref[0]
    ends = [jnp.minimum(starts[d + 1], used) if d + 1 < MAXDOC else used for d in range(MAXDOC)]
    patients = [pat_ref[0, d] for d in range(MAXDOC)]
    tile = (8, 128)
    sub8 = lax.broadcasted_iota(jnp.int32, tile, 0)
    lane8 = lax.broadcasted_iota(jnp.int32, tile, 1)
    own_hist = jnp.zeros(tile, F32)
    patient_of = jnp.zeros(tile, jnp.int32)
    for d in range(MAXDOC):
        nonempty = jnp.where(ends[d] > starts[d], 1.0, 0.0)
        own_hist = own_hist + jnp.where(lane8 == patients[d], nonempty, 0.0)
        patient_of = jnp.where(sub8 == d, patients[d], patient_of)
    hist[0, y] = own_hist

    def put_gram(which, block):
        low, high = pack_band(gram_of(block))
        for owner in range(NT):
            source = low if owner < 4 else high
            first = (owner % 4) * 16
            gp[owner, which] = source[first : first + 16].astype(GRAM_TYPE)

    loads[0].wait()
    xt[...] = xv[0].T
    put_gram(0, xv[0])
    loads[1].wait()
    put_gram(1, gy[0, y])
    loads[5].wait()
    loads[6].wait()
    for layer in range(1, LAYERS):
        put_gram(2 * layer, xv[layer])
        put_gram(2 * layer + 1, gv[layer - 1])

    pl.semaphore_wait(barrier, greetings + jnp.where(on_diagonal, 0, 2))

    sent = []

    def send(src, dst, send_sem, recv_sem, target):
        copy = remote(src, dst, send_sem, recv_sem, target)
        copy.start()
        sent.append(copy)

    def wait_for(slot, send_sem, recv_sem):
        remote(slot, slot, send_sem, recv_sem, sibling).wait_recv()

    def to_window(ref, send_sem, recv_sem):
        for wi, off in window_pairs:
            send(
                ref.at[0, y],
                ref.at[wi, y],
                send_sem.at[wi, off],
                recv_sem.at[wi, off],
                device(y_at(off), z_at(-WINDOW[wi]), x, c),
            )

    def from_window(ref, send_sem, recv_sem):
        for wi, off in window_pairs:
            wait_for(ref.at[wi, y_at(-off)], send_sem.at[wi, off], recv_sem.at[wi, off])

    def piece(wi, off):
        k = x_at(off)
        kind = lax.rem(z_at(-WINDOW[wi]), NW)
        first = k * PIECE
        row = 64 * (kind + NW * lax.div(first, 64)) + lax.rem(first, 64)
        return xt.at[pl.ds(pl.multiple_of(row, PIECE), PIECE)]

    def scatter(wi, off):
        k = x_at(off)
        return remote(
            piece(wi, off),
            xs.at[wi, y, k * 2 + c],
            sc_send.at[wi, off],
            sc_recv.at[wi, y],
            device(x, z_at(-WINDOW[wi]), k, c),
        )

    def grads_along_y(wi):
        block = gy.at[wi, y]
        send(block, block, gy_send.at[wi, 0], gy_recv.at[wi, 0], y_peer(1))
        send(block, block, gy_send.at[wi, 1], gy_recv.at[wi, 1], y_peer(-1))

    def grads_onward(wi):
        for way, step in ((0, 1), (1, -1)):
            block = gy.at[wi, y_at(-step)]
            wait_for(block, gy_send.at[wi, way], gy_recv.at[wi, way])
            half = gy.at[wi, y_at(-step), pl.ds(128 * way, 128)]
            send(half, half, gf_send.at[wi, way], gf_recv.at[wi, way], y_peer(step))

    to_window(hist, hist_send, hist_recv)

    own_piece = pltpu.make_async_copy(piece(0, 0), xs.at[0, y, tensor], sc_recv.at[0, y])
    own_scatter = scatter(0, 0)

    @pl.when(jnp.logical_not(on_diagonal))
    def _():
        own_scatter.start()

    @pl.when(on_diagonal)
    def _():
        own_piece.start()

    for wi, off in piece_pairs:
        copy = scatter(wi, off)
        copy.start()
        sent.append(copy)


    for off in range(1, NT):
        send(gp.at[t_at(off)], gr.at[tensor], gr_send.at[off], gr_recv.at[off], (dp, t_at(off)))

    for wi in range(1, NW):
        send(
            own_grads,
            gy.at[wi, y],
            gz_send.at[wi],
            gz_recv.at[wi],
            device(y, z_at(-WINDOW[wi]), x, c),
        )


    grads_along_y(0)

    from_window(hist, hist_send, hist_recv)
    window_count = hist[0, 0]
    for wi in range(NW):
        for yy in range(NY):
            if (wi, yy) != (0, 0):
                window_count = window_count + hist[wi, yy]
    ring[0] = window_count

    def ring_send_to(slot, src, target):
        send(ring.at[src], ring.at[slot], ring_send.at[slot], ring_recv.at[slot], target)

    def ring_wait(slot):
        wait_for(ring.at[slot], ring_send.at[slot], ring_recv.at[slot])

    for slot, target in ((3, below2), (4, above2), (1, below), (2, above)):
        ring_send_to(slot, 0, target)

    span = NW * NY // BLOCKS
    blocks = [(b * span // NY, b * span % NY) for b in range(BLOCKS)]

    def block_of(b, source_x, source_c):
        wi, first = blocks[b]
        return xs.at[wi, pl.ds(first, span), source_x * 2 + source_c]

    for b in range(BLOCKS // 2):
        wi, first = blocks[b]
        for yy in range(first, first + span):
            wait_for(xs.at[wi, yy, tensor], sc_send.at[0, 0], sc_recv.at[wi, yy])
        block = block_of(b, x, c)
        send(block, block, ag_send.at[0, b], ag_recv.at[0, b], x_peer(1))
        send(block, block, ag_send.at[1, b], ag_recv.at[1, b], x_peer(-1))
        send(block, block, sib_send.at[0, b], sib_recv.at[0, b], sibling)

    grads_onward(0)
    for b in range(BLOCKS // 2, BLOCKS):
        wi, first = blocks[b]
        for yy in range(first, first + span):
            wait_for(xs.at[wi, yy, tensor], sc_send.at[0, 0], sc_recv.at[wi, yy])
        block = block_of(b, x, c)
        send(block, block, ag_send.at[0, b], ag_recv.at[0, b], x_peer(1))
        send(block, block, ag_send.at[1, b], ag_recv.at[1, b], x_peer(-1))
        send(block, block, sib_send.at[0, b], sib_recv.at[0, b], sibling)

    for wi in range(1, NW):
        wait_for(gy.at[wi, y], gz_send.at[wi], gz_recv.at[wi])
        grads_along_y(wi)


    total = gp[tensor].astype(F32)
    for off in range(1, NT):
        source = t_at(-off)
        wait_for(gr.at[source], gr_send.at[off], gr_recv.at[off])
        total = total + gr[source].astype(F32)
    product = total[0] * total[1] + total[2] * total[3] + total[4] * total[5]
    band = (16, 128)
    packed_row = lax.broadcasted_iota(jnp.int32, band, 0) + tensor * 16
    packed_lane = lax.broadcasted_iota(jnp.int32, band, 1)
    inner_row = lax.rem(packed_row, 64)
    inner_lane = lax.rem(packed_lane, 64)
    base = 64 * (2 * lax.div(packed_row, 64) + lax.div(packed_lane, 64))
    tok_t = base + inner_row
    tok_s = base + inner_lane + jnp.where(inner_lane >= inner_row, 0, 64)
    product = product * jnp.where(tok_t == tok_s, 1.0, 2.0)
    norm_part = jnp.zeros(tile, F32)
    for d in range(MAXDOC):
        inside = (
            (tok_t >= starts[d]) & (tok_t < ends[d]) & (tok_s >= starts[d]) & (tok_s < ends[d])
        )
        value = jnp.sum(jnp.where(inside, product, 0.0), keepdims=True)
        norm_part = jnp.where(sub8 == d, value, norm_part)
    npr[tensor] = norm_part
    for off in range(1, NT):
        send(
            npr.at[tensor], npr.at[tensor], np_send.at[off], np_recv.at[off], (dp, t_at(off))
        )

    for slot in range(1, 5):
        ring_wait(slot)
    ring[5] = ring[1] + ring[3]
    ring_send_to(6, 5, below2)
    ring_send_to(7, 2, above2)

    for b in range(BLOCKS):
        for hop, step in ((0, 1), (1, -1)):
            block = block_of(b, x_at(-step), c)
            wait_for(block, ag_send.at[hop, b], ag_recv.at[hop, b])
            if (b < BLOCKS // 2) == (hop == 0):
                send(block, block, ag_send.at[2, b], ag_recv.at[2, b], x_peer(step))
            send(block, block, sib_send.at[hop + 1, b], sib_recv.at[hop + 1, b], sibling)

    for wi in range(1, NW):
        grads_onward(wi)

    ring_wait(6)
    ring_wait(7)
    counts = ring[0] + ring[6] + ring[7]
    for slot in range(1, 5):
        counts = counts + ring[slot]
    doc_count = jnp.sum(jnp.where(lane8 == patient_of, counts, 0.0), axis=1, keepdims=True)
    for off in range(1, NT):
        wait_for(npr.at[t_at(-off)], np_send.at[off], np_recv.at[off])
    norms = npr[0]
    for tt in range(1, NT):
        norms = norms + npr[tt]
    scale = clip_bound / jnp.maximum(clip_bound, jnp.sqrt(norms)) / jnp.maximum(doc_count, 1.0)
    position = lane8 + 128 * sub8
    weights = jnp.zeros(tile, F32)
    for d in range(MAXDOC):
        weights = jnp.where(
            (position >= starts[d]) & (position < ends[d]), scale[d : d + 1, :], weights
        )
    told[0, y] = weights
    to_window(told, told_send, told_recv)
    scale_row = jnp.sum(jnp.where(sub8 == lane8, scale, 0.0), axis=0, keepdims=True)
    scale_ref[...] = scale_row[:, :MAXDOC]

    for b in range(BLOCKS):
        block = block_of(b, x_at(2), c)
        wait_for(block, ag_send.at[2, b], ag_recv.at[2, b])
        send(block, block, sib_send.at[3, b], sib_recv.at[3, b], sibling)

    from_window(told, told_send, told_recv)
    columns = told[...].reshape(NW * NY * 8, 128).T
    for wi in range(NW):
        for way in range(2):
            half = gy.at[wi, y_at(2), pl.ds(128 * way, 128)]
            wait_for(half, gf_send.at[wi, way], gf_recv.at[wi, way])
        for yy in range(NY):
            for way in range(2):
                lane = (wi * NY + yy) * 8 + way
                rows = pl.ds(128 * way, 128)
                weight = columns[:, lane : lane + 1]
                wy[wi, yy, rows] = (weight * gy[wi, yy, rows].astype(F32)).astype(BF16)

    for hop, source_x in enumerate((x, x_at(-1), x_at(1), x_at(2))):
        for b in range(BLOCKS):
            wait_for(block_of(b, source_x, 1 - c), sib_send.at[hop, b], sib_recv.at[hop, b])

    sums = None
    for wi in range(NW):
        for yy in range(NY):
            features = xs[wi, yy].reshape(NT * PIECE, TOK)
            term = jnp.dot(features, wy[wi, yy], preferred_element_type=F32)
            sums = term if sums is None else sums + term
    step_rows = min(PIECE, 64)
    for tt in range(NT):
        for q in range(0, PIECE, step_rows):
            inner = (tt // 2) * PIECE + q
            owner = (tt % 2) * (8 // NW) + inner // 64
            first = tt * PIECE + q
            part[owner, inner % 64 : inner % 64 + step_rows] = sums[first : first + step_rows]

    rows = 64 // PIECES

    def owner_at(off):
        return lax.rem(place + off + members, members)

    def part_rows(off, j):
        return part.at[owner_at(off), pl.ds(j * rows, rows)]

    def arrival(slot, j):
        return sums_in.at[slot, pl.ds(j * rows, rows)]

    def sum_send(slot, j, off, target):
        send(
            part_rows(off, j),
            arrival(slot, j),
            sum_sent.at[slot, j],
            sum_recv.at[slot, j],
            target,
        )

    def sum_wait(slot, j):
        wait_for(arrival(slot, j), sum_sent.at[slot, j], sum_recv.at[slot, j])
        return arrival(slot, j)[...]

    for j in range(PIECES):
        if j % 2 == 0:
            sum_send(2, j, 4, below2)
        else:
            sum_send(3, j, 4, above2)
    for j in range(PIECES):
        sum_send(0, j, -3, below)
        sum_send(1, j, 3, above)
    for j in range(PIECES):
        sum_send(6, j, -1, below)
        sum_send(7, j, 1, above)

    for far in (False, True):
        for j in range(PIECES):
            for way in range(2):
                if far != (j % 2 == way):
                    continue
                near = (-2, 2)[way]
                value = sum_wait(way, j)
                if far:
                    value = value + sum_wait(2 + way, j)
                part_rows(near, j)[...] += value
                sum_send(4 + way, j, near, (below2, above2)[way])
    for j in range(PIECES):
        value = part[place, pl.ds(j * rows, rows), :]
        for slot in (6, 7, 4, 5):
            value = value + sum_wait(slot, j)
        out_ref[pl.ds(j * rows, rows), :] = value

    @pl.when(jnp.logical_not(on_diagonal))
    def _():
        own_scatter.wait_send()

    for copy in sent:
        copy.wait_send()


def on_device(nz, layer_inputs, layer_outgrads, doc_starts, row_tokens, doc_patient):
    clip_bound = DOC_MOST * math.sqrt(LAYERS * D * GW) / 300.0
    members = nz // NW
    assert members == 8
    vmem = pl.BlockSpec(memory_space=pltpu.VMEM)
    anywhere = pl.BlockSpec(memory_space=pl.ANY)
    dma = pltpu.SemaphoreType.DMA
    return pl.pallas_call(
        functools.partial(kernel, nz, clip_bound),
        out_shape=(
            jax.ShapeDtypeStruct((64, 256), F32),
            jax.ShapeDtypeStruct((1, MAXDOC), F32),
        ),
        in_specs=[anywhere] * 5,
        out_specs=(vmem, vmem),
        scratch_shapes=[
            pltpu.SMEM((1, MAXDOC), jnp.int32),
            pltpu.SMEM((1,), jnp.int32),
            pltpu.SMEM((1, MAXDOC), jnp.int32),
            pltpu.VMEM((LAYERS, TOK, 512), BF16),
            pltpu.VMEM((LAYERS - 1, TOK, 256), BF16),
            pltpu.VMEM((512, TOK), BF16),
            pltpu.VMEM((NW, NY, NT, PIECE, TOK), BF16),
            pltpu.VMEM((NW, NY, TOK, 256), BF16),
            pltpu.VMEM((NW, NY, TOK, 256), BF16),
            pltpu.VMEM((NT, 6, 16, 128), GRAM_TYPE),
            pltpu.VMEM((NT, 6, 16, 128), GRAM_TYPE),
            pltpu.VMEM((NT, 8, 128), F32),
            pltpu.VMEM((NW, NY, 8, 128), F32),
            pltpu.VMEM((8, 8, 128), F32),
            pltpu.VMEM((NW, NY, 8, 128), F32),
            pltpu.VMEM((members, 64, 256), F32),
            pltpu.VMEM((8, 64, 256), F32),
            dma((7,)),
            dma((NW, NX)),
            dma((NW, NY)),
            dma((NW,)),
            dma((NW,)),
            dma((NW, 2)),
            dma((NW, 2)),
            dma((NW, 2)),
            dma((NW, 2)),
            dma((NW, NY)),
            dma((NW, NY)),
            dma((8,)),
            dma((8,)),
            dma((NT,)),
            dma((NT,)),
            dma((NT,)),
            dma((NT,)),
            dma((NW, NY)),
            dma((NW, NY)),
            dma((3, BLOCKS)),
            dma((3, BLOCKS)),
            dma((4, BLOCKS)),
            dma((4, BLOCKS)),
            dma((8, PIECES)),
            dma((8, PIECES)),
        ],
        compiler_params=pltpu.CompilerParams(
            collective_id=0, has_side_effects=True, vmem_limit_bytes=VMEM_BYTES
        ),
    )(layer_inputs, layer_outgrads, doc_starts, row_tokens, doc_patient)


def solution(mesh):
    placed = (
        P(None, "dp", "tensor"),
        P(None, "dp", "tensor"),
        P("dp", None),
        P("dp"),
        P("dp", None),
    )
    return jax.shard_map(
        functools.partial(on_device, mesh.shape["dp"] // NY),
        mesh=mesh,
        in_specs=placed,
        out_specs=(P("dp", "tensor"), P("dp", None)),
        check_vma=False,
    )
```
